32 devices in a mesh: dp: 8 (over y, x, core), tensor: 4 (over z).
Axes of the slice: x: 2, y: 2, z: 4, core: 2. Of those that a mesh axis runs over, the one named last changes fastest.
Arguments:
- tokens: bfloat16 [1024, 64, 1024], P('tensor', 'dp'), may hold values from -1.6953125 to 1.6953125
- cond: bfloat16 [64, 1024], P('dp'), may hold values from -1.6953125 to 1.6953125
- cotangent: bfloat16 [1024, 64, 1024], P('tensor', 'dp'), may hold values from -1.6953125 to 1.6953125
- qkv_weight: bfloat16 [1024, 3, 1024], P(None, None, 'tensor'), may hold values from -0.1875 to 0.1875
- qv_bias: bfloat16 [2, 1024], P(None, 'tensor'), may hold values from -0.5 to 0.5
- output_projection_weight: bfloat16 [1024, 1024], P('tensor'), may hold values from -0.75 to 0.75
- proj_bias: bfloat16 [1024], replicated, may hold values from -0.5 to 0.5
- fc1_weight: bfloat16 [1024, 4096], P(None, 'tensor'), may hold values from -0.1875 to 0.1875
- fc1_bias: bfloat16 [4096], P('tensor'), may hold values from -0.5 to 0.5
- fc2_weight: bfloat16 [4096, 1024], P('tensor'), may hold values from -0.09375 to 0.09375
- fc2_bias: bfloat16 [1024], replicated, may hold values from -0.5 to 0.5
- ada_weight: bfloat16 [1024, 6, 1024], P(None, None, 'tensor'), may hold values from -0.1875 to 0.1875
- ada_bias: bfloat16 [6, 1024], P(None, 'tensor'), may hold values from -0.3984375 to 0.3984375
Outputs:
- output: bfloat16 [1024, 64, 1024], P('tensor', 'dp')
- grad_tokens: float32 [1024, 64, 1024], P('tensor', 'dp')
- grad_cond: float32 [64, 1024], P('dp')
- grad_qkv: float32 [1024, 3, 1024], P(None, None, 'tensor')
- grad_qv_bias: float32 [2, 1024], P(None, 'tensor')
- output_projection_gradient: float32 [1024, 1024], P('tensor')
- grad_proj_bias: float32 [1024], replicated
- grad_fc1: float32 [1024, 4096], P(None, 'tensor')
- grad_fc1_bias: float32 [4096], P('tensor')
- grad_fc2: float32 [4096, 1024], P('tensor')
- grad_fc2_bias: float32 [1024], replicated
- grad_ada: float32 [1024, 6, 1024], P(None, None, 'tensor')
- grad_ada_bias: float32 [6, 1024], P(None, 'tensor')
The draws below stay inside these ranges and needn't reach their ends.
All inputs are finite; a program needn't handle non-finite values.
Results may differ from the reference program's by a relative error of at most 0.02.
Values may be sent and summed in bfloat16 or wider, within the bound.
No kernel may reach another device: no remote copies, remote signals or barrier semaphores. Data moves between devices by JAX's collectives and lax.ppermute only.
A program may use at most 320 MiB of HBM per device.

```python
from functools import partial
import jax
import jax.numpy as jnp
from jax import lax

D = 1024
HEADS = 16
MLP = 4096
HD = 64
SEQ = 1024
LATENTS = 64


def shard_levels(key, extent, split, smallest, high):
    def one(axis_at, parts):
        heights = jax.random.uniform(jax.random.fold_in(jax.random.fold_in(key, 6), axis_at), (parts,), jnp.float32, smallest / len(split), high / len(split))
        return jnp.repeat(jnp.exp(heights), extent[axis_at] // parts).reshape((-1,) + (1,) * (len(extent) - axis_at - 1))

    gain = one(*split[0])
    for cut in split[1:]:
        gain = gain * one(*cut)
    return gain


def centred(rng, extent, scale, reach, shards=(), dtype=jnp.bfloat16):
    array = scale * jax.random.normal(rng, extent, jnp.float32)
    if shards:
        array = array * shard_levels(rng, extent, shards, -0.22, 0.18)
    return jnp.clip(array, -reach, reach).astype(dtype)


def setup_inputs(seed: int = 0) -> dict:
    key_list = jax.random.split(jax.random.key(seed), 14)
    return {
        "tokens": jnp.clip(jax.random.uniform(key_list[0], (SEQ, LATENTS, D), jnp.float32, -1.6953125, 1.6953125) * shard_levels(key_list[0], (SEQ, LATENTS, D), ((0, 4), (1, 8)), -0.4, 0.0), -1.6953125, 1.6953125).astype(jnp.bfloat16),
        "cond": jnp.clip(jax.random.uniform(key_list[1], (LATENTS, D), jnp.float32, -1.6953125, 1.6953125) * shard_levels(key_list[1], (LATENTS, D), ((0, 8),), -0.4, 0.0), -1.6953125, 1.6953125).astype(jnp.bfloat16),
        "cotangent": jnp.clip(jax.random.uniform(key_list[2], (SEQ, LATENTS, D), jnp.float32, -1.6953125, 1.6953125) * shard_levels(key_list[2], (SEQ, LATENTS, D), ((0, 4), (1, 8)), -0.4, 0.0), -1.6953125, 1.6953125).astype(jnp.bfloat16),
        "qkv_weight": centred(key_list[3], (D, 3, D), D ** -0.5, 0.1875, ((2, 4),)),
        "qv_bias": jnp.clip(jax.random.uniform(key_list[4], (2, D), jnp.float32, -0.5, 0.5) * shard_levels(key_list[4], (2, D), ((1, 4),), -0.4, 0.0), -0.5, 0.5).astype(jnp.bfloat16),
        "output_projection_weight": centred(key_list[5], (D, D), (D // 16) ** -0.5, 0.75, ((0, 4),)),
        "proj_bias": jnp.clip(jax.random.uniform(key_list[6], (D,), jnp.float32, -0.5, 0.5), -0.5, 0.5).astype(jnp.bfloat16),
        "fc1_weight": centred(key_list[7], (D, MLP), D ** -0.5, 0.1875, ((1, 4),)),
        "fc1_bias": jnp.clip(jax.random.uniform(key_list[8], (MLP,), jnp.float32, -0.5, 0.5) * shard_levels(key_list[8], (MLP,), ((0, 4),), -0.4, 0.0), -0.5, 0.5).astype(jnp.bfloat16),
        "fc2_weight": centred(key_list[9], (MLP, D), MLP ** -0.5, 0.09375, ((0, 4),)),
        "fc2_bias": jnp.clip(jax.random.uniform(key_list[10], (D,), jnp.float32, -0.5, 0.5), -0.5, 0.5).astype(jnp.bfloat16),
        "ada_weight": centred(key_list[11], (D, 6, D), D ** -0.5, 0.1875, ((2, 4),)),
        "ada_bias": jnp.clip(jax.random.uniform(key_list[12], (6, D), jnp.float32, -0.3984375, 0.3984375) * shard_levels(key_list[12], (6, D), ((1, 4),), -0.4, 0.0), -0.3984375, 0.3984375).astype(jnp.bfloat16),
    }


@jax.custom_vjp
def low(v):
    return lax.optimization_barrier(v.astype(jnp.bfloat16)).astype(jnp.float32)

@jax.custom_vjp
def low_back(v):
    return v

def low_keep(v):
    return (low(v), None)

def low_pass(kept, grad):
    return (grad,)

def back_keep(v):
    return (v, None)

def back_low(kept, grad):
    return (low(grad),)
low.defvjp(low_keep, low_pass)
low_back.defvjp(back_keep, back_low)

def matmul(left, right):
    return jnp.dot(left, right, precision=lax.Precision.HIGHEST)

def layer_stats(values):
    row_mean = lax.optimization_barrier(jnp.mean(values, -1, keepdims=True))
    centered = values - row_mean
    variance = lax.optimization_barrier(jnp.mean(centered * centered, -1, keepdims=True))
    return centered * lax.rsqrt(variance + 1e-06)

def one_latent(weights, latent):
    tokens, cond = latent
    qkv_weight, qv_bias, output_projection_weight, proj_bias, fc1_weight, fc1_bias, fc2_weight, fc2_bias, ada_weight, ada_bias = weights
    silu_c = low(jax.nn.silu(cond))
    modulation = low(matmul(silu_c[None], ada_weight.reshape(D, 6 * D))[0] + ada_bias.reshape(6 * D)).reshape(6, D)
    shift1, scale1, gate1, shift2, scale2, gate2 = [modulation[index] for index in range(6)]
    attn_in = low(layer_stats(tokens) * (1.0 + scale1) + shift1)
    projected = matmul(attn_in, qkv_weight.reshape(D, 3 * D)).reshape(SEQ, 3, D)
    queries = low(low_back(projected[:, 0] + qv_bias[0])).reshape(SEQ, HEADS, HD)
    keys_all = low(low_back(projected[:, 1])).reshape(SEQ, HEADS, HD)
    values_all = low(low_back(projected[:, 2] + qv_bias[1])).reshape(SEQ, HEADS, HD)
    scores = low_back(jnp.einsum('qhd,khd->hqk', queries, keys_all, precision=lax.Precision.HIGHEST) * HD ** (-0.5))
    probs = low(jax.nn.softmax(scores, axis=-1))
    attention_result = jnp.einsum('hqk,khd->qhd', probs, values_all, precision=lax.Precision.HIGHEST).reshape(SEQ, D)
    attention_result = low(low_back(attention_result))
    attn_out = low_back(matmul(attention_result, output_projection_weight) + proj_bias)
    mid = tokens + gate1 * attn_out
    feedforward_input = low(layer_stats(mid) * (1.0 + scale2) + shift2)
    pre = low_back(matmul(feedforward_input, fc1_weight) + fc1_bias)
    gelu_activation = low(jax.nn.gelu(pre, approximate=True))
    mlp_out = low_back(matmul(gelu_activation, fc2_weight) + fc2_bias)
    return mid + gate2 * mlp_out

def forward(tokens, cond, qkv_weight, qv_bias, output_projection_weight, proj_bias, fc1_weight, fc1_bias, fc2_weight, fc2_bias, ada_weight, ada_bias):
    weights = (qkv_weight, qv_bias, output_projection_weight, proj_bias, fc1_weight, fc1_bias, fc2_weight, fc2_bias, ada_weight, ada_bias)
    per_latent = jnp.transpose(tokens, (1, 0, 2))
    results = lax.map(jax.checkpoint(partial(one_latent, weights)), (per_latent, cond))
    return jnp.transpose(results, (1, 0, 2))

def reference(tokens, cond, cotangent, qkv_weight, qv_bias, output_projection_weight, proj_bias, fc1_weight, fc1_bias, fc2_weight, fc2_bias, ada_weight, ada_bias):
    inputs = [item.astype(jnp.float32) for item in (tokens, cond, qkv_weight, qv_bias, output_projection_weight, proj_bias, fc1_weight, fc1_bias, fc2_weight, fc2_bias, ada_weight, ada_bias)]
    output, pullback = jax.vjp(forward, inputs[0], inputs[1], inputs[2], inputs[3], inputs[4], inputs[5], inputs[6], inputs[7], inputs[8], inputs[9], inputs[10], inputs[11])
    grads = pullback(cotangent.astype(jnp.float32))
    return (output.astype(jnp.bfloat16), grads[0], grads[1], grads[2], grads[3], grads[4], grads[5], grads[6], grads[7], grads[8], grads[9], grads[10], grads[11])
```

```python
from functools import partial

import jax
import jax.numpy as jnp
from jax import lax
from jax.experimental import pallas as pl
from jax.experimental.pallas import tpu as pltpu
from jax.sharding import PartitionSpec as P

HD = 64
LANES = 128


def layer_stats(values):
    row_mean = jnp.mean(values, -1, keepdims=True)
    centered = values - row_mean
    variance = jnp.mean(centered * centered, -1, keepdims=True)
    inverse = lax.rsqrt(variance + 1e-06)
    return (centered * inverse, inverse)


def norm_back(d_norm, normed, inverse):
    first = jnp.mean(d_norm, -1, keepdims=True)
    second = jnp.mean(d_norm * normed, -1, keepdims=True)
    return inverse * (d_norm - first - normed * second)


def split_heads(
    tokens,
    cond,
    cotangent,
    qkv_weight,
    qv_bias,
    output_projection_weight,
    proj_bias,
    fc1_weight,
    fc1_bias,
    fc2_weight,
    fc2_bias,
    ada_weight,
    ada_bias,
):
    row_count, latents, model_width = tokens.shape
    local_width = qkv_weight.shape[2]
    heads_local = local_width // HD
    seq_len = row_count * lax.axis_size("tensor")
    factor = HD ** (-0.5)

    def to_heads(array):
        return jnp.transpose(array.reshape(seq_len, latents, heads_local, HD), (1, 2, 0, 3))

    def from_heads(array):
        return jnp.transpose(array, (2, 0, 1, 3)).reshape(seq_len, latents, local_width)

    def attend(block):
        query_blk, key_blk, value_blk = block
        scores = (
            jnp.einsum("hqd,hkd->hqk", query_blk, key_blk, preferred_element_type=jnp.float32)
            * factor
        )
        row_max = jnp.max(scores, -1, keepdims=True)
        log_total = row_max + jnp.log(jnp.sum(jnp.exp(scores - row_max), -1, keepdims=True))
        probs = jnp.exp(scores - log_total).astype(jnp.bfloat16)
        result = jnp.einsum("hqk,hkd->hqd", probs, value_blk, preferred_element_type=jnp.float32)
        return (result.astype(jnp.bfloat16), log_total[..., 0])

    def attend_back(block):
        query_blk, key_blk, value_blk, log_total, grad_blk = block
        scores = (
            jnp.einsum("hqd,hkd->hqk", query_blk, key_blk, preferred_element_type=jnp.float32)
            * factor
        )
        weights = jnp.exp(scores - log_total[..., None])
        d_probs = jnp.einsum(
            "hqd,hkd->hqk", grad_blk, value_blk, preferred_element_type=jnp.float32
        )
        d_scores = (weights * (d_probs - jnp.sum(d_probs * weights, -1, keepdims=True))).astype(
            jnp.bfloat16
        )
        d_query = (
            jnp.einsum("hqk,hkd->hqd", d_scores, key_blk, preferred_element_type=jnp.float32)
            * factor
        ).astype(jnp.bfloat16)
        d_key = (
            jnp.einsum("hqk,hqd->hkd", d_scores, query_blk, preferred_element_type=jnp.float32)
            * factor
        ).astype(jnp.bfloat16)
        d_value = jnp.einsum(
            "hqk,hqd->hkd",
            weights.astype(jnp.bfloat16),
            grad_blk,
            preferred_element_type=jnp.float32,
        ).astype(jnp.bfloat16)
        return (d_query, d_key, d_value)

    cond_float = cond.astype(jnp.float32)
    silu_c = jax.nn.silu(cond_float).astype(jnp.bfloat16)
    ada_flat = ada_weight.reshape(model_width, 6 * local_width)
    mod_part = jnp.dot(silu_c, ada_flat, preferred_element_type=jnp.float32) + ada_bias.reshape(
        6 * local_width
    ).astype(jnp.float32)
    mod_part = mod_part.reshape(latents, 6, local_width).astype(jnp.bfloat16)
    modulation = lax.all_gather(mod_part, "tensor", axis=2, tiled=True).astype(jnp.float32)
    shift1, scale1, gate1, shift2, scale2, gate2 = [
        modulation[:, index][None] for index in range(6)
    ]
    first_dense_weight_gathered, second_dense_weight_gathered, fc1_bias_full = (
        lax.all_gather(fc1_weight, "tensor", axis=1, tiled=True),
        lax.all_gather(fc2_weight, "tensor", axis=0, tiled=True),
        lax.all_gather(fc1_bias, "tensor", axis=0, tiled=True),
    )
    inputs_float = tokens.astype(jnp.float32)
    norm1, inverse1 = layer_stats(inputs_float)
    attn_in = (norm1 * (1.0 + scale1) + shift1).astype(jnp.bfloat16)
    attention_gathered = lax.all_gather(attn_in, "tensor", axis=0, tiled=True)
    query_key_value_rows = qkv_weight.reshape(model_width, 3 * local_width)
    projected = jnp.einsum(
        "rap,po->rao", attention_gathered, query_key_value_rows, preferred_element_type=jnp.float32
    ).reshape(seq_len, latents, 3, local_width)
    bias_float = qv_bias.astype(jnp.float32)
    queries = to_heads((projected[:, :, 0] + bias_float[0]).astype(jnp.bfloat16))
    keys_all = to_heads(projected[:, :, 1].astype(jnp.bfloat16))
    values_all = to_heads((projected[:, :, 2] + bias_float[1]).astype(jnp.bfloat16))
    attended_heads, log_totals = lax.map(attend, (queries, keys_all, values_all))
    attention_result = from_heads(attended_heads)
    shard_slice = attention_result
    attn_out = lax.psum_scatter(
        jnp.einsum(
            "pac,cx->pax", shard_slice, output_projection_weight, preferred_element_type=jnp.float32
        ).astype(jnp.bfloat16),
        "tensor",
        scatter_dimension=0,
        tiled=True,
    ).astype(jnp.float32) + proj_bias.astype(jnp.float32)
    mid = inputs_float + gate1 * attn_out
    norm2, inverse2 = layer_stats(mid)
    feedforward_input = (norm2 * (1.0 + scale2) + shift2).astype(jnp.bfloat16)
    pre = jnp.einsum(
        "biw,wr->bir",
        feedforward_input,
        first_dense_weight_gathered,
        preferred_element_type=jnp.float32,
    ) + fc1_bias_full.astype(jnp.float32)
    gelu_activation = jax.nn.gelu(pre, approximate=True).astype(jnp.bfloat16)
    mlp_out = jnp.einsum(
        "gzw,wt->gzt",
        gelu_activation,
        second_dense_weight_gathered,
        preferred_element_type=jnp.float32,
    ) + fc2_bias.astype(jnp.float32)
    output = (mid + gate2 * mlp_out).astype(jnp.bfloat16)
    grad_out = cotangent.astype(jnp.float32)
    grad_gate2 = jnp.sum(grad_out * mlp_out, 0)
    feedforward_gradient = (grad_out * gate2).astype(jnp.bfloat16)
    fc2_bias_part = jnp.sum(feedforward_gradient.astype(jnp.float32), (0, 1))
    second_dense_gradient_shard = jnp.einsum(
        "rqu,rqf->uf", gelu_activation, feedforward_gradient, preferred_element_type=jnp.float32
    )
    activation_gradient = jnp.einsum(
        "zqy,vy->zqv",
        feedforward_gradient,
        second_dense_weight_gathered,
        preferred_element_type=jnp.float32,
    )
    gelu_pull = jax.vjp(partial(jax.nn.gelu, approximate=True), pre)[1]
    preactivation_gradient = gelu_pull(activation_gradient)[0].astype(jnp.bfloat16)
    fc1_bias_part = jnp.sum(preactivation_gradient.astype(jnp.float32), (0, 1))
    first_dense_gradient_shard = jnp.einsum(
        "hic,hip->cp", feedforward_input, preactivation_gradient, preferred_element_type=jnp.float32
    )
    feedforward_input_gradient = jnp.einsum(
        "xfg,yg->xfy",
        preactivation_gradient,
        first_dense_weight_gathered,
        preferred_element_type=jnp.float32,
    )
    grad_fc1, grad_fc2, grad_fc1_bias = (
        lax.psum_scatter(
            first_dense_gradient_shard.astype(jnp.bfloat16),
            "tensor",
            scatter_dimension=1,
            tiled=True,
        ).astype(jnp.float32),
        lax.psum_scatter(
            second_dense_gradient_shard.astype(jnp.bfloat16),
            "tensor",
            scatter_dimension=0,
            tiled=True,
        ).astype(jnp.float32),
        lax.psum_scatter(
            fc1_bias_part.astype(jnp.bfloat16), "tensor", scatter_dimension=0, tiled=True
        ).astype(jnp.float32),
    )
    grad_shift2 = jnp.sum(feedforward_input_gradient, 0)
    grad_scale2 = jnp.sum(feedforward_input_gradient * norm2, 0)
    d_mid = grad_out + norm_back(feedforward_input_gradient * (1.0 + scale2), norm2, inverse2)
    grad_gate1 = jnp.sum(d_mid * attn_out, 0)
    d_attn = (d_mid * gate1).astype(jnp.bfloat16)
    proj_bias_part = jnp.sum(d_attn.astype(jnp.float32), (0, 1))
    attention_gathered_gradient = lax.all_gather(d_attn, "tensor", axis=0, tiled=True)
    output_projection_gradient = jnp.einsum(
        "pti,ptq->iq",
        attention_result,
        attention_gathered_gradient,
        preferred_element_type=jnp.float32,
    )
    d_attended = jnp.einsum(
        "btw,vw->btv",
        attention_gathered_gradient,
        output_projection_weight,
        preferred_element_type=jnp.float32,
    ).astype(jnp.bfloat16)
    d_query_h, d_key_h, d_value_h = lax.map(
        attend_back, (queries, keys_all, values_all, log_totals, to_heads(d_attended))
    )
    d_queries = from_heads(d_query_h)
    d_values = from_heads(d_value_h)
    query_key_value_gradient = jnp.stack([d_queries, from_heads(d_key_h), d_values], 2).reshape(
        seq_len, latents, 3 * local_width
    )
    grad_qv_bias = jnp.stack(
        [
            jnp.sum(d_queries.astype(jnp.float32), (0, 1)),
            jnp.sum(d_values.astype(jnp.float32), (0, 1)),
        ],
        0,
    )
    grad_qkv = jnp.einsum(
        "iyz,iyn->zn",
        attention_gathered,
        query_key_value_gradient,
        preferred_element_type=jnp.float32,
    ).reshape(model_width, 3, local_width)
    shard_slice = query_key_value_gradient
    d_attn_in = lax.psum_scatter(
        jnp.einsum(
            "rnt,mt->rnm", shard_slice, query_key_value_rows, preferred_element_type=jnp.float32
        ).astype(jnp.bfloat16),
        "tensor",
        scatter_dimension=0,
        tiled=True,
    ).astype(jnp.float32)
    grad_shift1 = jnp.sum(d_attn_in, 0)
    grad_scale1 = jnp.sum(d_attn_in * norm1, 0)
    grad_tokens = d_mid + norm_back(d_attn_in * (1.0 + scale1), norm1, inverse1)
    d_modulation = jnp.stack(
        [grad_shift1, grad_scale1, grad_gate1, grad_shift2, grad_scale2, grad_gate2], 1
    )
    d_mod_local = lax.psum_scatter(
        d_modulation.astype(jnp.bfloat16), "tensor", scatter_dimension=2, tiled=True
    ).astype(jnp.float32)
    grad_ada_bias = jnp.sum(d_mod_local, 0)
    d_mod_flat = d_mod_local.reshape(latents, 6 * local_width)
    grad_ada = jnp.dot(
        silu_c.astype(jnp.float32).T, d_mod_flat, precision=lax.Precision.HIGHEST
    ).reshape(model_width, 6, local_width)
    d_silu_part = jnp.dot(
        d_mod_flat, ada_flat.astype(jnp.float32).T, precision=lax.Precision.HIGHEST
    )
    d_silu, grad_fc2_bias, grad_proj_bias = (
        lax.psum(d_silu_part.astype(jnp.bfloat16), "tensor").astype(jnp.float32),
        lax.psum(fc2_bias_part.astype(jnp.bfloat16), "tensor").astype(jnp.float32),
        lax.psum(proj_bias_part.astype(jnp.bfloat16), "tensor").astype(jnp.float32),
    )
    silu_pull = jax.vjp(jax.nn.silu, cond_float)[1]
    grad_cond = silu_pull(d_silu)[0]
    (
        grad_qkv,
        grad_qv_bias,
        output_projection_gradient,
        grad_proj_bias,
        grad_fc1,
        grad_fc1_bias,
        grad_fc2,
        grad_fc2_bias,
        grad_ada,
        grad_ada_bias,
    ) = (
        lax.psum(grad_qkv.astype(jnp.bfloat16), "dp").astype(jnp.float32),
        lax.psum(grad_qv_bias.astype(jnp.bfloat16), "dp").astype(jnp.float32),
        lax.psum(output_projection_gradient.astype(jnp.bfloat16), "dp").astype(jnp.float32),
        lax.psum(grad_proj_bias.astype(jnp.bfloat16), "dp").astype(jnp.float32),
        lax.psum(grad_fc1.astype(jnp.bfloat16), "dp").astype(jnp.float32),
        lax.psum(grad_fc1_bias.astype(jnp.bfloat16), "dp").astype(jnp.float32),
        lax.psum(grad_fc2.astype(jnp.bfloat16), "dp").astype(jnp.float32),
        lax.psum(grad_fc2_bias.astype(jnp.bfloat16), "dp").astype(jnp.float32),
        lax.psum(grad_ada.astype(jnp.bfloat16), "dp").astype(jnp.float32),
        lax.psum(grad_ada_bias.astype(jnp.bfloat16), "dp").astype(jnp.float32),
    )
    return (
        output,
        grad_tokens,
        grad_cond,
        grad_qkv,
        grad_qv_bias,
        output_projection_gradient,
        grad_proj_bias,
        grad_fc1,
        grad_fc1_bias,
        grad_fc2,
        grad_fc2_bias,
        grad_ada,
        grad_ada_bias,
    )


def _nt(left, right):
    return lax.dot_general(
        left, right, (((1,), (1,)), ((), ())), preferred_element_type=jnp.float32
    )


def _attend_kernel(qkv_ref, out_ref, lse_ref, *, width, rows):
    lane = lax.broadcasted_iota(jnp.int32, (1, LANES), 1)
    first = lane < HD

    def chunk(index, carry):
        at = pl.ds(pl.multiple_of(index * rows, rows), rows)
        totals = jnp.zeros((rows, LANES), jnp.float32)
        for pair in range(width // LANES):
            lo = pair * LANES
            query = qkv_ref[at, lo : lo + LANES] * jnp.bfloat16(HD**-0.5)
            key = qkv_ref[:, width + lo : width + lo + LANES]
            value = qkv_ref[:, 2 * width + lo : 2 * width + lo + LANES]
            parts = []
            for side in range(2):
                mine = first if side == 0 else jnp.logical_not(first)
                scores = _nt(jnp.where(mine, query, 0), key)
                top = jnp.max(scores, -1, keepdims=True)
                weights = jnp.exp(scores - top).astype(jnp.bfloat16)
                mixed = jnp.dot(
                    weights, jnp.where(mine, value, 1), preferred_element_type=jnp.float32
                )
                other = HD * (1 - side)
                total = mixed[:, other : other + 1]
                parts.append(mixed / total)
                totals = jnp.where(lane == 2 * pair + side, top + jnp.log(total), totals)
            out_ref[at, lo : lo + LANES] = jnp.where(first, parts[0], parts[1]).astype(
                jnp.bfloat16
            )
        lse_ref[at, :] = totals
        return carry

    lax.fori_loop(0, qkv_ref.shape[0] // rows, chunk, 0)


def attend(qkv, latents, groups, width, seq):
    heads = groups * (width // HD)
    work = latents * heads * seq * seq
    return pl.pallas_call(
        partial(_attend_kernel, width=width, rows=min(256, seq)),
        grid=(latents, groups),
        in_specs=[pl.BlockSpec((seq, 3 * width), lambda i, j: (i, j))],
        out_specs=[
            pl.BlockSpec((seq, width), lambda i, j: (i, j)),
            pl.BlockSpec((seq, LANES), lambda i, j: (i, j)),
        ],
        out_shape=[
            jax.ShapeDtypeStruct((latents * seq, groups * width), jnp.bfloat16),
            jax.ShapeDtypeStruct((latents * seq, groups * LANES), jnp.float32),
        ],
        compiler_params=pltpu.CompilerParams(vmem_limit_bytes=40 * 2**20),
        cost_estimate=pl.CostEstimate(
            flops=16 * HD * work,
            bytes_accessed=latents * seq * groups * (8 * width + 4 * LANES),
            transcendentals=work,
        ),
        name="attend",
    )(qkv)


def _split3(column):
    high = column.astype(jnp.bfloat16).astype(jnp.float32)
    middle = (column - high).astype(jnp.bfloat16).astype(jnp.float32)
    return (high, middle, column - high - middle)


def _attend_back_kernel(qkv_ref, out_ref, lse_ref, grad_ref, dqkv_ref, *, width, rows):
    seq = qkv_ref.shape[0]
    lane = lax.broadcasted_iota(jnp.int32, (1, LANES), 1)
    first = lane < HD
    scale = jnp.bfloat16(HD**-0.5)

    def extend(mine, base, array, column):
        high, middle, low = _split3(column)
        extra = jnp.where(
            lane == base,
            high,
            jnp.where(lane == base + 1, middle, jnp.where(lane == base + 2, low, 0.0)),
        )
        return jnp.where(mine, array, extra.astype(jnp.bfloat16))

    for pair in range(width // LANES):
        lo = pair * LANES
        query = qkv_ref[:, lo : lo + LANES] * scale
        grad = grad_ref[:, lo : lo + LANES]
        product = grad.astype(jnp.float32) * out_ref[:, lo : lo + LANES].astype(jnp.float32)
        queries, grads = [], []
        for side in range(2):
            mine = first if side == 0 else jnp.logical_not(first)
            base = HD * (1 - side)
            head = 2 * pair + side
            queries.append(extend(mine, base, query, -lse_ref[:, head : head + 1]))
            inner = jnp.sum(jnp.where(mine, product, 0.0), -1, keepdims=True)
            grads.append(extend(mine, base, grad, -inner))
        d_query = [jnp.zeros((HD, seq), jnp.float32)] * 2
        for index in range(seq // rows):
            at = slice(index * rows, (index + 1) * rows)
            key = qkv_ref[at, width + lo : width + lo + LANES]
            value = qkv_ref[at, 2 * width + lo : 2 * width + lo + LANES]
            key_t = key.T
            d_key, d_value = [], []
            for side in range(2):
                mine = first if side == 0 else jnp.logical_not(first)
                base = HD * (1 - side)
                ones = jnp.where((lane >= base) & (lane < base + 3), 1.0, 0.0).astype(jnp.bfloat16)
                weights = jnp.exp(_nt(jnp.where(mine, key, ones), queries[side]))
                d_scores = (
                    weights * _nt(jnp.where(mine, value, ones), grads[side])
                ).astype(jnp.bfloat16)
                d_value.append(
                    jnp.dot(
                        weights.astype(jnp.bfloat16), grad, preferred_element_type=jnp.float32
                    )
                )
                d_key.append(jnp.dot(d_scores, query, preferred_element_type=jnp.float32))
                d_query[side] = d_query[side] + jnp.dot(
                    key_t[side * HD : (side + 1) * HD],
                    d_scores,
                    preferred_element_type=jnp.float32,
                )
            dqkv_ref[at, width + lo : width + lo + LANES] = jnp.where(
                first, d_key[0], d_key[1]
            ).astype(jnp.bfloat16)
            dqkv_ref[at, 2 * width + lo : 2 * width + lo + LANES] = jnp.where(
                first, d_value[0], d_value[1]
            ).astype(jnp.bfloat16)
        d_query_t = jnp.concatenate(d_query, 0) * (HD**-0.5)
        dqkv_ref[:, lo : lo + LANES] = d_query_t.T.astype(jnp.bfloat16)


def attend_back(qkv, out, lse, grad, latents, groups, width, seq):
    heads = groups * (width // HD)
    work = latents * heads * seq * seq
    return pl.pallas_call(
        partial(_attend_back_kernel, width=width, rows=min(256, seq)),
        grid=(latents, groups),
        in_specs=[
            pl.BlockSpec((seq, 3 * width), lambda i, j: (i, j)),
            pl.BlockSpec((seq, width), lambda i, j: (i, j)),
            pl.BlockSpec((seq, LANES), lambda i, j: (i, j)),
            pl.BlockSpec((seq, width), lambda i, j: (i, j)),
        ],
        out_specs=pl.BlockSpec((seq, 3 * width), lambda i, j: (i, j)),
        out_shape=jax.ShapeDtypeStruct(qkv.shape, jnp.bfloat16),
        compiler_params=pltpu.CompilerParams(vmem_limit_bytes=48 * 2**20),
        cost_estimate=pl.CostEstimate(
            flops=40 * HD * work,
            bytes_accessed=latents * seq * groups * (16 * width + 4 * LANES),
            transcendentals=work,
        ),
        name="attend_back",
    )(qkv, out, lse, grad)


BY_OWNER, BY_SHARE = ("tensor", "dp"), ("dp", "tensor")


def exchange(pieces):
    return lax.all_to_all(pieces, "tensor", 0, 0)


def gather_rows(part, order):
    share = part.shape[0] // lax.axis_size("dp")
    mine = lax.dynamic_slice_in_dim(part, lax.axis_index("dp") * share, share, 0)
    return lax.all_gather(mine, order, axis=0, tiled=True)


def by_share(rows):
    groups, shares = lax.axis_size("tensor"), lax.axis_size("dp")
    split = rows.reshape(groups, shares, -1, *rows.shape[1:])
    return jnp.swapaxes(split, 0, 1).reshape(rows.shape)


def sum_rows(whole):
    share = lax.psum_scatter(
        whole.astype(jnp.bfloat16), "dp", scatter_dimension=0, tiled=True
    )
    share = lax.psum_scatter(share, "tensor", scatter_dimension=0, tiled=True)
    return lax.all_gather(share, "dp", axis=0, tiled=True).astype(jnp.float32)


def whole_latents(
    tokens,
    cond,
    cotangent,
    qkv_weight,
    qv_bias,
    output_projection_weight,
    proj_bias,
    fc1_weight,
    fc1_bias,
    fc2_weight,
    fc2_bias,
    ada_weight,
    ada_bias,
):
    row_count, group_latents, model_width = tokens.shape
    groups = lax.axis_size("tensor")
    latents = group_latents // groups
    seq = row_count * groups
    width = qkv_weight.shape[2]
    hidden = fc1_weight.shape[1]
    rows = latents * seq
    me = lax.axis_index("tensor")

    def to_latents(array):
        pieces = jnp.transpose(
            array.reshape(row_count, groups, latents, model_width), (1, 2, 0, 3)
        )
        return jnp.transpose(exchange(pieces), (1, 0, 2, 3)).reshape(latents, seq, model_width)

    def to_tokens(array):
        pieces = jnp.transpose(
            array.reshape(latents, groups, row_count, model_width), (1, 0, 2, 3)
        )
        return jnp.transpose(exchange(pieces), (2, 0, 1, 3)).reshape(
            row_count, group_latents, model_width
        )

    cond_float = cond.astype(jnp.float32)
    silu_c = jax.nn.silu(cond_float).astype(jnp.bfloat16)
    ada_flat = ada_weight.reshape(model_width, 6 * width)
    mod_part = jnp.dot(silu_c, ada_flat, preferred_element_type=jnp.float32) + ada_bias.reshape(
        6 * width
    ).astype(jnp.float32)
    mod_part = mod_part.reshape(group_latents, 6, width).astype(jnp.bfloat16)
    modulation = lax.dynamic_slice_in_dim(
        lax.all_gather(mod_part, "tensor", axis=2, tiled=True), me * latents, latents, 0
    ).astype(jnp.float32)
    shift1, scale1, gate1, shift2, scale2, gate2 = [
        modulation[:, index][:, None] for index in range(6)
    ]

    qkv_rows = gather_rows(
        jnp.transpose(qkv_weight, (1, 2, 0)).reshape(3 * width, model_width),
        BY_OWNER,
    )
    inputs_float = to_latents(tokens).astype(jnp.float32)
    proj_rows = gather_rows(output_projection_weight, BY_OWNER)
    fc1_rows = gather_rows(fc1_weight.T, BY_SHARE)
    fc2_rows = gather_rows(fc2_weight, BY_SHARE)
    fc1_bias_full = by_share(
        lax.all_gather(fc1_bias, "tensor", axis=0, tiled=True)
    ).astype(jnp.float32)
    qv_bias_full = lax.all_gather(qv_bias, "tensor", axis=0).astype(jnp.float32)
    qkv_bias = jnp.stack(
        [qv_bias_full[:, 0], jnp.zeros_like(qv_bias_full[:, 0]), qv_bias_full[:, 1]], 1
    ).reshape(groups * 3 * width)
    grad_out = to_latents(cotangent).astype(jnp.float32)

    norm1, inverse1 = layer_stats(inputs_float)
    attn_in = (norm1 * (1.0 + scale1) + shift1).astype(jnp.bfloat16).reshape(rows, model_width)
    qkv = (_nt(attn_in, qkv_rows) + qkv_bias).astype(jnp.bfloat16)
    attended, log_totals = attend(qkv, latents, groups, width, seq)
    attn_out = (
        jnp.dot(attended, proj_rows, preferred_element_type=jnp.float32)
        + proj_bias.astype(jnp.float32)
    ).reshape(latents, seq, model_width)
    mid = inputs_float + gate1 * attn_out
    norm2, inverse2 = layer_stats(mid)
    mlp_in = (norm2 * (1.0 + scale2) + shift2).astype(jnp.bfloat16).reshape(rows, model_width)
    pre = _nt(mlp_in, fc1_rows) + fc1_bias_full
    act = jax.nn.gelu(pre, approximate=True).astype(jnp.bfloat16)
    mlp_out = (
        jnp.dot(act, fc2_rows, preferred_element_type=jnp.float32) + fc2_bias.astype(jnp.float32)
    ).reshape(latents, seq, model_width)
    output = to_tokens((mid + gate2 * mlp_out).astype(jnp.bfloat16))

    grad_gate2 = jnp.sum(grad_out * mlp_out, 1)
    d_mlp = (grad_out * gate2).astype(jnp.bfloat16).reshape(rows, model_width)
    fc2_bias_part = jnp.sum(d_mlp.astype(jnp.float32), 0)
    grad_fc2 = sum_rows(
        lax.dot_general(act, d_mlp, (((0,), (0,)), ((), ())), preferred_element_type=jnp.float32)
    )
    d_act = _nt(d_mlp, fc2_rows)
    d_pre = jax.vjp(partial(jax.nn.gelu, approximate=True), pre)[1](d_act)[0].astype(jnp.bfloat16)
    fc1_bias_part = jnp.sum(d_pre.astype(jnp.float32), 0)
    grad_fc1 = sum_rows(
        lax.dot_general(d_pre, mlp_in, (((0,), (0,)), ((), ())), preferred_element_type=jnp.float32)
    ).T
    d_mlp_in = jnp.dot(d_pre, fc1_rows, preferred_element_type=jnp.float32).reshape(
        latents, seq, model_width
    )
    grad_shift2 = jnp.sum(d_mlp_in, 1)
    grad_scale2 = jnp.sum(d_mlp_in * norm2, 1)
    d_mid = grad_out + norm_back(d_mlp_in * (1.0 + scale2), norm2, inverse2)
    grad_gate1 = jnp.sum(d_mid * attn_out, 1)
    d_attn = (d_mid * gate1).astype(jnp.bfloat16).reshape(rows, model_width)
    proj_bias_part = jnp.sum(d_attn.astype(jnp.float32), 0)
    grad_proj = sum_rows(
        by_share(
            lax.dot_general(
                attended, d_attn, (((0,), (0,)), ((), ())), preferred_element_type=jnp.float32
            )
        )
    )
    d_attended = _nt(d_attn, proj_rows).astype(jnp.bfloat16)
    d_qkv = attend_back(qkv, attended, log_totals, d_attended, latents, groups, width, seq)
    qkv_bias_part = jnp.sum(d_qkv.astype(jnp.float32), 0)
    grad_qkv = jnp.transpose(
        sum_rows(
            by_share(
                lax.dot_general(
                    d_qkv, attn_in, (((0,), (0,)), ((), ())), preferred_element_type=jnp.float32
                )
            )
        ).reshape(3, width, model_width),
        (2, 0, 1),
    )
    d_attn_in = jnp.dot(d_qkv, qkv_rows, preferred_element_type=jnp.float32).reshape(
        latents, seq, model_width
    )
    grad_shift1 = jnp.sum(d_attn_in, 1)
    grad_scale1 = jnp.sum(d_attn_in * norm1, 1)
    grad_tokens = to_tokens(
        (d_mid + norm_back(d_attn_in * (1.0 + scale1), norm1, inverse1)).astype(jnp.bfloat16)
    ).astype(jnp.float32)

    d_modulation = jnp.stack(
        [grad_shift1, grad_scale1, grad_gate1, grad_shift2, grad_scale2, grad_gate2], 1
    ).astype(jnp.bfloat16)
    d_mod_group = lax.all_to_all(d_modulation, "tensor", 2, 0, tiled=True).reshape(
        group_latents, 6 * width
    )
    d_mod_all = lax.all_gather(d_mod_group, "dp", axis=0, tiled=True)
    cond_all = lax.all_gather(cond, "dp", axis=0, tiled=True)
    silu_all = jax.nn.silu(cond_all.astype(jnp.float32)).astype(jnp.bfloat16)
    grad_ada_bias = jnp.sum(d_mod_all.astype(jnp.float32), 0).reshape(6, width)
    grad_ada = lax.dot_general(
        silu_all, d_mod_all, (((0,), (0,)), ((), ())), preferred_element_type=jnp.float32
    ).reshape(model_width, 6, width)
    d_silu = lax.psum(_nt(d_mod_group, ada_flat).astype(jnp.bfloat16), "tensor").astype(
        jnp.float32
    )
    grad_cond = jax.vjp(jax.nn.silu, cond_float)[1](d_silu)[0]

    biases = lax.psum(
        jnp.concatenate([fc2_bias_part, proj_bias_part, fc1_bias_part, qkv_bias_part]).astype(
            jnp.bfloat16
        ),
        ("dp", "tensor"),
    ).astype(jnp.float32)
    grad_fc2_bias = biases[:model_width]
    grad_proj_bias = biases[model_width : 2 * model_width]
    at = 2 * model_width
    grad_fc1_bias = lax.dynamic_slice_in_dim(
        biases[at : at + hidden * groups].reshape(-1, groups, hidden // lax.axis_size("dp")),
        me,
        1,
        1,
    ).reshape(hidden)
    at = at + hidden * groups
    grad_qv_bias = lax.dynamic_slice_in_dim(biases, at + me * 3 * width, 3 * width, 0).reshape(
        3, width
    )[::2]
    return (
        output,
        grad_tokens,
        grad_cond,
        grad_qkv,
        grad_qv_bias,
        grad_proj,
        grad_proj_bias,
        grad_fc1,
        grad_fc1_bias,
        grad_fc2,
        grad_fc2_bias,
        grad_ada,
        grad_ada_bias,
    )


def shards(tokens, cond, cotangent, qkv_weight, *rest):
    even = tokens.shape[1] % lax.axis_size("tensor") == 0 and qkv_weight.shape[2] % LANES == 0
    program = whole_latents if even else split_heads
    return program(tokens, cond, cotangent, qkv_weight, *rest)


def solution(mesh):
    return jax.shard_map(
        shards,
        mesh=mesh,
        in_specs=(
            P("tensor", "dp", None),
            P("dp", None),
            P("tensor", "dp", None),
            P(None, None, "tensor"),
            P(None, "tensor"),
            P("tensor", None),
            P(),
            P(None, "tensor"),
            P("tensor"),
            P("tensor", None),
            P(),
            P(None, None, "tensor"),
            P(None, "tensor"),
        ),
        out_specs=(
            P("tensor", "dp", None),
            P("tensor", "dp", None),
            P("dp", None),
            P(None, None, "tensor"),
            P(None, "tensor"),
            P("tensor", None),
            P(),
            P(None, "tensor"),
            P("tensor"),
            P("tensor", None),
            P(),
            P(None, None, "tensor"),
            P(None, "tensor"),
        ),
        check_vma=False,
    )
```

```python
from functools import partial

import jax
import jax.numpy as jnp
from jax import lax
from jax.experimental import pallas as pl
from jax.experimental.pallas import tpu as pltpu
from jax.sharding import PartitionSpec as P

HD = 64
LANES = 128


def layer_stats(values):
    row_mean = jnp.mean(values, -1, keepdims=True)
    centered = values - row_mean
    variance = jnp.mean(centered * centered, -1, keepdims=True)
    inverse = lax.rsqrt(variance + 1e-06)
    return (centered * inverse, inverse)


def norm_back(d_norm, normed, inverse):
    first = jnp.mean(d_norm, -1, keepdims=True)
    second = jnp.mean(d_norm * normed, -1, keepdims=True)
    return inverse * (d_norm - first - normed * second)


def split_heads(
    tokens,
    cond,
    cotangent,
    qkv_weight,
    qv_bias,
    output_projection_weight,
    proj_bias,
    fc1_weight,
    fc1_bias,
    fc2_weight,
    fc2_bias,
    ada_weight,
    ada_bias,
):
    row_count, latents, model_width = tokens.shape
    local_width = qkv_weight.shape[2]
    heads_local = local_width // HD
    seq_len = row_count * lax.axis_size("tensor")
    factor = HD ** (-0.5)

    def to_heads(array):
        return jnp.transpose(array.reshape(seq_len, latents, heads_local, HD), (1, 2, 0, 3))

    def from_heads(array):
        return jnp.transpose(array, (2, 0, 1, 3)).reshape(seq_len, latents, local_width)

    def attend(block):
        query_blk, key_blk, value_blk = block
        scores = (
            jnp.einsum("hqd,hkd->hqk", query_blk, key_blk, preferred_element_type=jnp.float32)
            * factor
        )
        row_max = jnp.max(scores, -1, keepdims=True)
        log_total = row_max + jnp.log(jnp.sum(jnp.exp(scores - row_max), -1, keepdims=True))
        probs = jnp.exp(scores - log_total).astype(jnp.bfloat16)
        result = jnp.einsum("hqk,hkd->hqd", probs, value_blk, preferred_element_type=jnp.float32)
        return (result.astype(jnp.bfloat16), log_total[..., 0])

    def attend_back(block):
        query_blk, key_blk, value_blk, log_total, grad_blk = block
        scores = (
            jnp.einsum("hqd,hkd->hqk", query_blk, key_blk, preferred_element_type=jnp.float32)
            * factor
        )
        weights = jnp.exp(scores - log_total[..., None])
        d_probs = jnp.einsum(
            "hqd,hkd->hqk", grad_blk, value_blk, preferred_element_type=jnp.float32
        )
        d_scores = (weights * (d_probs - jnp.sum(d_probs * weights, -1, keepdims=True))).astype(
            jnp.bfloat16
        )
        d_query = (
            jnp.einsum("hqk,hkd->hqd", d_scores, key_blk, preferred_element_type=jnp.float32)
            * factor
        ).astype(jnp.bfloat16)
        d_key = (
            jnp.einsum("hqk,hqd->hkd", d_scores, query_blk, preferred_element_type=jnp.float32)
            * factor
        ).astype(jnp.bfloat16)
        d_value = jnp.einsum(
            "hqk,hqd->hkd",
            weights.astype(jnp.bfloat16),
            grad_blk,
            preferred_element_type=jnp.float32,
        ).astype(jnp.bfloat16)
        return (d_query, d_key, d_value)

    cond_float = cond.astype(jnp.float32)
    silu_c = jax.nn.silu(cond_float).astype(jnp.bfloat16)
    ada_flat = ada_weight.reshape(model_width, 6 * local_width)
    mod_part = jnp.dot(silu_c, ada_flat, preferred_element_type=jnp.float32) + ada_bias.reshape(
        6 * local_width
    ).astype(jnp.float32)
    mod_part = mod_part.reshape(latents, 6, local_width).astype(jnp.bfloat16)
    modulation = lax.all_gather(mod_part, "tensor", axis=2, tiled=True).astype(jnp.float32)
    shift1, scale1, gate1, shift2, scale2, gate2 = [
        modulation[:, index][None] for index in range(6)
    ]
    first_dense_weight_gathered, second_dense_weight_gathered, fc1_bias_full = (
        lax.all_gather(fc1_weight, "tensor", axis=1, tiled=True),
        lax.all_gather(fc2_weight, "tensor", axis=0, tiled=True),
        lax.all_gather(fc1_bias, "tensor", axis=0, tiled=True),
    )
    inputs_float = tokens.astype(jnp.float32)
    norm1, inverse1 = layer_stats(inputs_float)
    attn_in = (norm1 * (1.0 + scale1) + shift1).astype(jnp.bfloat16)
    attention_gathered = lax.all_gather(attn_in, "tensor", axis=0, tiled=True)
    query_key_value_rows = qkv_weight.reshape(model_width, 3 * local_width)
    projected = jnp.einsum(
        "rap,po->rao", attention_gathered, query_key_value_rows, preferred_element_type=jnp.float32
    ).reshape(seq_len, latents, 3, local_width)
    bias_float = qv_bias.astype(jnp.float32)
    queries = to_heads((projected[:, :, 0] + bias_float[0]).astype(jnp.bfloat16))
    keys_all = to_heads(projected[:, :, 1].astype(jnp.bfloat16))
    values_all = to_heads((projected[:, :, 2] + bias_float[1]).astype(jnp.bfloat16))
    attended_heads, log_totals = lax.map(attend, (queries, keys_all, values_all))
    attention_result = from_heads(attended_heads)
    shard_slice = attention_result
    attn_out = lax.psum_scatter(
        jnp.einsum(
            "pac,cx->pax", shard_slice, output_projection_weight, preferred_element_type=jnp.float32
        ).astype(jnp.bfloat16),
        "tensor",
        scatter_dimension=0,
        tiled=True,
    ).astype(jnp.float32) + proj_bias.astype(jnp.float32)
    mid = inputs_float + gate1 * attn_out
    norm2, inverse2 = layer_stats(mid)
    feedforward_input = (norm2 * (1.0 + scale2) + shift2).astype(jnp.bfloat16)
    pre = jnp.einsum(
        "biw,wr->bir",
        feedforward_input,
        first_dense_weight_gathered,
        preferred_element_type=jnp.float32,
    ) + fc1_bias_full.astype(jnp.float32)
    gelu_activation = jax.nn.gelu(pre, approximate=True).astype(jnp.bfloat16)
    mlp_out = jnp.einsum(
        "gzw,wt->gzt",
        gelu_activation,
        second_dense_weight_gathered,
        preferred_element_type=jnp.float32,
    ) + fc2_bias.astype(jnp.float32)
    output = (mid + gate2 * mlp_out).astype(jnp.bfloat16)
    grad_out = cotangent.astype(jnp.float32)
    grad_gate2 = jnp.sum(grad_out * mlp_out, 0)
    feedforward_gradient = (grad_out * gate2).astype(jnp.bfloat16)
    fc2_bias_part = jnp.sum(feedforward_gradient.astype(jnp.float32), (0, 1))
    second_dense_gradient_shard = jnp.einsum(
        "rqu,rqf->uf", gelu_activation, feedforward_gradient, preferred_element_type=jnp.float32
    )
    activation_gradient = jnp.einsum(
        "zqy,vy->zqv",
        feedforward_gradient,
        second_dense_weight_gathered,
        preferred_element_type=jnp.float32,
    )
    gelu_pull = jax.vjp(partial(jax.nn.gelu, approximate=True), pre)[1]
    preactivation_gradient = gelu_pull(activation_gradient)[0].astype(jnp.bfloat16)
    fc1_bias_part = jnp.sum(preactivation_gradient.astype(jnp.float32), (0, 1))
    first_dense_gradient_shard = jnp.einsum(
        "hic,hip->cp", feedforward_input, preactivation_gradient, preferred_element_type=jnp.float32
    )
    feedforward_input_gradient = jnp.einsum(
        "xfg,yg->xfy",
        preactivation_gradient,
        first_dense_weight_gathered,
        preferred_element_type=jnp.float32,
    )
    grad_fc1, grad_fc2, grad_fc1_bias = (
        lax.psum_scatter(
            first_dense_gradient_shard.astype(jnp.bfloat16),
            "tensor",
            scatter_dimension=1,
            tiled=True,
        ).astype(jnp.float32),
        lax.psum_scatter(
            second_dense_gradient_shard.astype(jnp.bfloat16),
            "tensor",
            scatter_dimension=0,
            tiled=True,
        ).astype(jnp.float32),
        lax.psum_scatter(
            fc1_bias_part.astype(jnp.bfloat16), "tensor", scatter_dimension=0, tiled=True
        ).astype(jnp.float32),
    )
    grad_shift2 = jnp.sum(feedforward_input_gradient, 0)
    grad_scale2 = jnp.sum(feedforward_input_gradient * norm2, 0)
    d_mid = grad_out + norm_back(feedforward_input_gradient * (1.0 + scale2), norm2, inverse2)
    grad_gate1 = jnp.sum(d_mid * attn_out, 0)
    d_attn = (d_mid * gate1).astype(jnp.bfloat16)
    proj_bias_part = jnp.sum(d_attn.astype(jnp.float32), (0, 1))
    attention_gathered_gradient = lax.all_gather(d_attn, "tensor", axis=0, tiled=True)
    output_projection_gradient = jnp.einsum(
        "pti,ptq->iq",
        attention_result,
        attention_gathered_gradient,
        preferred_element_type=jnp.float32,
    )
    d_attended = jnp.einsum(
        "btw,vw->btv",
        attention_gathered_gradient,
        output_projection_weight,
        preferred_element_type=jnp.float32,
    ).astype(jnp.bfloat16)
    d_query_h, d_key_h, d_value_h = lax.map(
        attend_back, (queries, keys_all, values_all, log_totals, to_heads(d_attended))
    )
    d_queries = from_heads(d_query_h)
    d_values = from_heads(d_value_h)
    query_key_value_gradient = jnp.stack([d_queries, from_heads(d_key_h), d_values], 2).reshape(
        seq_len, latents, 3 * local_width
    )
    grad_qv_bias = jnp.stack(
        [
            jnp.sum(d_queries.astype(jnp.float32), (0, 1)),
            jnp.sum(d_values.astype(jnp.float32), (0, 1)),
        ],
        0,
    )
    grad_qkv = jnp.einsum(
        "iyz,iyn->zn",
        attention_gathered,
        query_key_value_gradient,
        preferred_element_type=jnp.float32,
    ).reshape(model_width, 3, local_width)
    shard_slice = query_key_value_gradient
    d_attn_in = lax.psum_scatter(
        jnp.einsum(
            "rnt,mt->rnm", shard_slice, query_key_value_rows, preferred_element_type=jnp.float32
        ).astype(jnp.bfloat16),
        "tensor",
        scatter_dimension=0,
        tiled=True,
    ).astype(jnp.float32)
    grad_shift1 = jnp.sum(d_attn_in, 0)
    grad_scale1 = jnp.sum(d_attn_in * norm1, 0)
    grad_tokens = d_mid + norm_back(d_attn_in * (1.0 + scale1), norm1, inverse1)
    d_modulation = jnp.stack(
        [grad_shift1, grad_scale1, grad_gate1, grad_shift2, grad_scale2, grad_gate2], 1
    )
    d_mod_local = lax.psum_scatter(
        d_modulation.astype(jnp.bfloat16), "tensor", scatter_dimension=2, tiled=True
    ).astype(jnp.float32)
    grad_ada_bias = jnp.sum(d_mod_local, 0)
    d_mod_flat = d_mod_local.reshape(latents, 6 * local_width)
    grad_ada = jnp.dot(
        silu_c.astype(jnp.float32).T, d_mod_flat, precision=lax.Precision.HIGHEST
    ).reshape(model_width, 6, local_width)
    d_silu_part = jnp.dot(
        d_mod_flat, ada_flat.astype(jnp.float32).T, precision=lax.Precision.HIGHEST
    )
    d_silu, grad_fc2_bias, grad_proj_bias = (
        lax.psum(d_silu_part.astype(jnp.bfloat16), "tensor").astype(jnp.float32),
        lax.psum(fc2_bias_part.astype(jnp.bfloat16), "tensor").astype(jnp.float32),
        lax.psum(proj_bias_part.astype(jnp.bfloat16), "tensor").astype(jnp.float32),
    )
    silu_pull = jax.vjp(jax.nn.silu, cond_float)[1]
    grad_cond = silu_pull(d_silu)[0]
    (
        grad_qkv,
        grad_qv_bias,
        output_projection_gradient,
        grad_proj_bias,
        grad_fc1,
        grad_fc1_bias,
        grad_fc2,
        grad_fc2_bias,
        grad_ada,
        grad_ada_bias,
    ) = (
        lax.psum(grad_qkv.astype(jnp.bfloat16), "dp").astype(jnp.float32),
        lax.psum(grad_qv_bias.astype(jnp.bfloat16), "dp").astype(jnp.float32),
        lax.psum(output_projection_gradient.astype(jnp.bfloat16), "dp").astype(jnp.float32),
        lax.psum(grad_proj_bias.astype(jnp.bfloat16), "dp").astype(jnp.float32),
        lax.psum(grad_fc1.astype(jnp.bfloat16), "dp").astype(jnp.float32),
        lax.psum(grad_fc1_bias.astype(jnp.bfloat16), "dp").astype(jnp.float32),
        lax.psum(grad_fc2.astype(jnp.bfloat16), "dp").astype(jnp.float32),
        lax.psum(grad_fc2_bias.astype(jnp.bfloat16), "dp").astype(jnp.float32),
        lax.psum(grad_ada.astype(jnp.bfloat16), "dp").astype(jnp.float32),
        lax.psum(grad_ada_bias.astype(jnp.bfloat16), "dp").astype(jnp.float32),
    )
    return (
        output,
        grad_tokens,
        grad_cond,
        grad_qkv,
        grad_qv_bias,
        output_projection_gradient,
        grad_proj_bias,
        grad_fc1,
        grad_fc1_bias,
        grad_fc2,
        grad_fc2_bias,
        grad_ada,
        grad_ada_bias,
    )


def _nt(left, right):
    return lax.dot_general(
        left, right, (((1,), (1,)), ((), ())), preferred_element_type=jnp.float32
    )


def _attend_kernel(qkv_ref, out_ref, lse_ref, *, width, rows):
    lane = lax.broadcasted_iota(jnp.int32, (1, LANES), 1)
    first = lane < HD

    def chunk(index, carry):
        at = pl.ds(pl.multiple_of(index * rows, rows), rows)
        totals = jnp.zeros((rows, LANES), jnp.float32)
        for pair in range(width // LANES):
            lo = pair * LANES
            query = qkv_ref[at, lo : lo + LANES] * jnp.bfloat16(HD**-0.5)
            key = qkv_ref[:, width + lo : width + lo + LANES]
            value = qkv_ref[:, 2 * width + lo : 2 * width + lo + LANES]
            parts = []
            for side in range(2):
                mine = first if side == 0 else jnp.logical_not(first)
                scores = _nt(jnp.where(mine, query, 0), key)
                top = jnp.max(scores, -1, keepdims=True)
                weights = jnp.exp(scores - top).astype(jnp.bfloat16)
                mixed = jnp.dot(
                    weights, jnp.where(mine, value, 1), preferred_element_type=jnp.float32
                )
                other = HD * (1 - side)
                total = mixed[:, other : other + 1]
                parts.append(mixed / total)
                totals = jnp.where(lane == 2 * pair + side, top + jnp.log(total), totals)
            out_ref[at, lo : lo + LANES] = jnp.where(first, parts[0], parts[1]).astype(
                jnp.bfloat16
            )
        lse_ref[at, :] = totals
        return carry

    lax.fori_loop(0, qkv_ref.shape[0] // rows, chunk, 0)


def attend(qkv, latents, groups, width, seq):
    heads = groups * (width // HD)
    work = latents * heads * seq * seq
    return pl.pallas_call(
        partial(_attend_kernel, width=width, rows=min(256, seq)),
        grid=(latents, groups),
        in_specs=[pl.BlockSpec((seq, 3 * width), lambda i, j: (i, j))],
        out_specs=[
            pl.BlockSpec((seq, width), lambda i, j: (i, j)),
            pl.BlockSpec((seq, LANES), lambda i, j: (i, j)),
        ],
        out_shape=[
            jax.ShapeDtypeStruct((latents * seq, groups * width), jnp.bfloat16),
            jax.ShapeDtypeStruct((latents * seq, groups * LANES), jnp.float32),
        ],
        compiler_params=pltpu.CompilerParams(vmem_limit_bytes=40 * 2**20),
        cost_estimate=pl.CostEstimate(
            flops=16 * HD * work,
            bytes_accessed=latents * seq * groups * (8 * width + 4 * LANES),
            transcendentals=work,
        ),
        name="attend",
    )(qkv)


def _split3(column):
    high = column.astype(jnp.bfloat16).astype(jnp.float32)
    middle = (column - high).astype(jnp.bfloat16).astype(jnp.float32)
    return (high, middle, column - high - middle)


def _attend_back_kernel(qkv_ref, out_ref, lse_ref, grad_ref, dqkv_ref, *, width, rows):
    seq = qkv_ref.shape[0]
    lane = lax.broadcasted_iota(jnp.int32, (1, LANES), 1)
    first = lane < HD
    scale = jnp.bfloat16(HD**-0.5)

    def extend(mine, base, array, column):
        high, middle, low = _split3(column)
        extra = jnp.where(
            lane == base,
            high,
            jnp.where(lane == base + 1, middle, jnp.where(lane == base + 2, low, 0.0)),
        )
        return jnp.where(mine, array, extra.astype(jnp.bfloat16))

    for pair in range(width // LANES):
        lo = pair * LANES
        query = qkv_ref[:, lo : lo + LANES] * scale
        grad = grad_ref[:, lo : lo + LANES]
        product = grad.astype(jnp.float32) * out_ref[:, lo : lo + LANES].astype(jnp.float32)
        queries, grads = [], []
        for side in range(2):
            mine = first if side == 0 else jnp.logical_not(first)
            base = HD * (1 - side)
            head = 2 * pair + side
            queries.append(extend(mine, base, query, -lse_ref[:, head : head + 1]))
            inner = jnp.sum(jnp.where(mine, product, 0.0), -1, keepdims=True)
            grads.append(extend(mine, base, grad, -inner))
        d_query = [jnp.zeros((HD, seq), jnp.float32)] * 2
        for index in range(seq // rows):
            at = slice(index * rows, (index + 1) * rows)
            key = qkv_ref[at, width + lo : width + lo + LANES]
            value = qkv_ref[at, 2 * width + lo : 2 * width + lo + LANES]
            key_t = key.T
            d_key, d_value = [], []
            for side in range(2):
                mine = first if side == 0 else jnp.logical_not(first)
                base = HD * (1 - side)
                ones = jnp.where((lane >= base) & (lane < base + 3), 1.0, 0.0).astype(jnp.bfloat16)
                weights = jnp.exp(_nt(jnp.where(mine, key, ones), queries[side]))
                d_scores = (
                    weights * _nt(jnp.where(mine, value, ones), grads[side])
                ).astype(jnp.bfloat16)
                d_value.append(
                    jnp.dot(
                        weights.astype(jnp.bfloat16), grad, preferred_element_type=jnp.float32
                    )
                )
                d_key.append(jnp.dot(d_scores, query, preferred_element_type=jnp.float32))
                d_query[side] = d_query[side] + jnp.dot(
                    key_t[side * HD : (side + 1) * HD],
                    d_scores,
                    preferred_element_type=jnp.float32,
                )
            dqkv_ref[at, width + lo : width + lo + LANES] = jnp.where(
                first, d_key[0], d_key[1]
            ).astype(jnp.bfloat16)
            dqkv_ref[at, 2 * width + lo : 2 * width + lo + LANES] = jnp.where(
                first, d_value[0], d_value[1]
            ).astype(jnp.bfloat16)
        d_query_t = jnp.concatenate(d_query, 0) * (HD**-0.5)
        dqkv_ref[:, lo : lo + LANES] = d_query_t.T.astype(jnp.bfloat16)


def attend_back(qkv, out, lse, grad, latents, groups, width, seq):
    heads = groups * (width // HD)
    work = latents * heads * seq * seq
    return pl.pallas_call(
        partial(_attend_back_kernel, width=width, rows=min(256, seq)),
        grid=(latents, groups),
        in_specs=[
            pl.BlockSpec((seq, 3 * width), lambda i, j: (i, j)),
            pl.BlockSpec((seq, width), lambda i, j: (i, j)),
            pl.BlockSpec((seq, LANES), lambda i, j: (i, j)),
            pl.BlockSpec((seq, width), lambda i, j: (i, j)),
        ],
        out_specs=pl.BlockSpec((seq, 3 * width), lambda i, j: (i, j)),
        out_shape=jax.ShapeDtypeStruct(qkv.shape, jnp.bfloat16),
        compiler_params=pltpu.CompilerParams(vmem_limit_bytes=48 * 2**20),
        cost_estimate=pl.CostEstimate(
            flops=40 * HD * work,
            bytes_accessed=latents * seq * groups * (16 * width + 4 * LANES),
            transcendentals=work,
        ),
        name="attend_back",
    )(qkv, out, lse, grad)


SHARES, GROUPS = 8, 4


def xor_permute(array, axis, mask):
    size = lax.axis_size(axis)
    return lax.ppermute(array, axis, [(index, index ^ mask) for index in range(size)])


def xor_order(array, index, axes):
    for place, axis in enumerate(reversed(axes)):
        array = jnp.where((index >> place) & 1 == 1, jnp.flip(array, axis), array)
    return array


def add_low(left, right):
    return (left.astype(jnp.float32) + right.astype(jnp.float32)).astype(jnp.bfloat16)


def _merge_kernel(*refs):
    *piece_refs, array_ref = refs
    pieces = [ref[member] for member in range(GROUPS) for ref in piece_refs]
    array_ref[...] = jnp.swapaxes(
        jnp.stack([piece.astype(jnp.float32) for piece in pieces], 0), 0, 1
    ).astype(array_ref.dtype)


def merge_latents(pieces, dtype):
    _, count, depth = pieces[0].shape
    step, latents = 32, len(pieces)
    size = GROUPS * latents * count * depth
    return pl.pallas_call(
        _merge_kernel,
        grid=(count // step,),
        in_specs=[pl.BlockSpec((GROUPS, step, depth), lambda i: (0, i, 0))] * latents,
        out_specs=pl.BlockSpec((step, GROUPS * latents, depth), lambda i: (i, 0, 0)),
        out_shape=jax.ShapeDtypeStruct((count, GROUPS * latents, depth), dtype),
        cost_estimate=pl.CostEstimate(flops=0, bytes_accessed=6 * size, transcendentals=0),
        name="merge_latents",
    )(*pieces)


class Flow:
    def __init__(self, stages):
        self.stages, self.result = stages, None
        self.values = next(stages)

    def advance(self, values):
        try:
            self.values = self.stages.send(values)
        except StopIteration as stop:
            self.values, self.result = (), stop.value


def window(compute, *flows):
    compute, values = lax.optimization_barrier((compute, [flow.values for flow in flows]))
    for flow, value in zip(flows, values):
        flow.advance(value)
    return compute


def sent(array, move):
    array = yield move(array)
    return array


def gather_local(mine, shares, pauses):
    place = lax.axis_index("dp")
    near, far = xor_permute(mine, "tensor", 1), xor_permute(mine, "tensor", 2)
    got = (near, far, xor_permute(far, "tensor", 1))
    if 0 in pauses:
        got = yield got
    block = jnp.stack(got, 0)
    half = mine.shape[0] // 2
    along_x, along_y = xor_permute(block, "dp", 2), xor_permute(block, "dp", 4)
    other = xor_permute(block, "dp", 1)
    if 1 in pauses:
        block, along_x, along_y, other = yield (block, along_x, along_y, other)
    halves = [xor_permute(along_x[:, :half], "dp", 4), xor_permute(along_y[:, half:], "dp", 2)]
    others = [other, xor_permute(along_x, "dp", 1), xor_permute(along_y, "dp", 1)]
    if 2 in pauses:
        halves, others = yield (halves, others)
    across = jnp.concatenate(halves, 1)
    chips = [block, along_x, along_y, across]
    blocks = yield [chips, [*others, xor_permute(across, "dp", 1)]]
    return [
        [
            jnp.concatenate(
                [
                    lax.dynamic_index_in_dim(shares, place ^ (2 * chip + core), 0),
                    blocks[core][chip],
                ],
                0,
            )
            for chip in range(4)
        ]
        for core in range(2)
    ]


def reduce_local(blocks, pauses):
    half = blocks.shape[3] // 2
    pair = (blocks[0], xor_permute(blocks[1], "dp", 1))
    if 0 in pauses:
        pair = yield pair
    total = add_low(*pair)
    total = total.reshape(2, 2, *total.shape[1:])
    first, second = total[:, :, :, :half], total[:, :, :, half:]
    pairs = (
        (first[:, 0], xor_permute(first[:, 1], "dp", 2)),
        (second[0], xor_permute(second[1], "dp", 4)),
    )
    if 1 in pauses:
        pairs = yield pairs
    first, second = [add_low(*pair) for pair in pairs]
    pairs = (
        (first[0], xor_permute(first[1], "dp", 4)),
        (second[0], xor_permute(second[1], "dp", 2)),
    )
    if 2 in pauses:
        pairs = yield pairs
    total = jnp.concatenate([add_low(*pair) for pair in pairs], 1)
    total = total.reshape(2, 2, *total.shape[1:])
    total = add_low(total[:, 0], xor_permute(total[:, 1], "tensor", 1))
    pair = (total[0], xor_permute(total[1], "tensor", 2))
    pair = yield pair
    return add_low(*pair)


def gathered(*shares):
    sizes = [share.shape[0] for share in shares]
    share = jnp.concatenate(shares, 0) if len(shares) > 1 else shares[0]
    whole = yield lax.all_gather(share, "dp", axis=0)
    parts, at = [], 0
    for size in sizes:
        parts.append(whole[:, at : at + size])
        at += size
    return parts


def group_send(pieces):
    return [pieces[0]] + [xor_permute(pieces[mask], "tensor", mask) for mask in range(1, GROUPS)]


def group_add(pieces):
    first, second, third, fourth = [piece.astype(jnp.float32) for piece in pieces]
    return (first + second) + (third + fourth)


def whole_latents(
    tokens,
    cond,
    cotangent,
    qkv_weight,
    qv_bias,
    output_projection_weight,
    proj_bias,
    fc1_weight,
    fc1_bias,
    fc2_weight,
    fc2_bias,
    ada_weight,
    ada_bias,
):
    row_count, group_latents, model_width = tokens.shape
    latents = group_latents // GROUPS
    seq = row_count * GROUPS
    width = qkv_weight.shape[2]
    hidden = fc1_weight.shape[1]
    rows = latents * seq
    part, slot = hidden // SHARES, width // SHARES
    me, place = lax.axis_index("tensor"), lax.axis_index("dp")

    def split_tokens(array):
        pieces = jnp.transpose(
            array.reshape(row_count, GROUPS, latents, model_width), (1, 2, 0, 3)
        )
        return [pieces[:, index] for index in range(latents)]

    def exchange(pieces):
        return lax.all_to_all(pieces, "tensor", 0, 0)

    def contract(left, right):
        return lax.dot_general(
            left, right, (((0,), (0,)), ((), ())), preferred_element_type=jnp.float32
        )

    qkv_t = jnp.transpose(qkv_weight.reshape(model_width, 3, SHARES, slot), (2, 1, 3, 0))
    attention_shares = jnp.concatenate(
        [
            qkv_t.reshape(SHARES, 3 * slot, model_width),
            output_projection_weight.reshape(SHARES, slot, model_width),
        ],
        1,
    )
    own_qkv = lax.dynamic_index_in_dim(
        qkv_weight.reshape(model_width, 3, SHARES, slot), place, 2, keepdims=False
    )
    own_attention = jnp.concatenate(
        [
            jnp.transpose(own_qkv, (1, 2, 0)).reshape(3 * slot, model_width),
            lax.dynamic_slice_in_dim(output_projection_weight, place * slot, slot, 0),
        ],
        0,
    )
    weights = Flow(gather_local(own_attention, attention_shares, (0,)))
    pieces = window(split_tokens(tokens), weights)
    incoming = [Flow(sent(pieces[0], exchange))]
    grad_pieces = split_tokens(cotangent)
    fc1_shares = fc1_weight.T.reshape(SHARES, part, model_width)
    fc2_shares = fc2_weight.reshape(SHARES, part, model_width)
    own_fc1 = lax.dynamic_index_in_dim(fc1_shares, place, 0, keepdims=False)
    own_fc2 = lax.dynamic_index_in_dim(fc2_shares, place, 0, keepdims=False)

    cond_float = cond.astype(jnp.float32)
    silu_c = jax.nn.silu(cond_float).astype(jnp.bfloat16)
    ada_flat = ada_weight.reshape(model_width, 6 * width)
    mod_part = jnp.dot(silu_c, ada_flat, preferred_element_type=jnp.float32) + ada_bias.reshape(
        6 * width
    ).astype(jnp.float32)
    mod_part = mod_part.astype(jnp.bfloat16).reshape(GROUPS, latents, 6, width)
    mod_got = []
    for mask in range(GROUPS):
        piece = lax.dynamic_index_in_dim(mod_part, me ^ mask, 0, keepdims=False)
        mod_got.append(xor_permute(piece, "tensor", mask) if mask else piece)
    modulation = xor_order(jnp.stack(mod_got, 0).reshape(2, 2, latents, 6, width), me, (0, 1))
    modulation = jnp.transpose(
        modulation.reshape(GROUPS, latents, 6, width), (1, 2, 0, 3)
    ).reshape(latents, 6, model_width)
    own_biases = jnp.concatenate([fc1_bias, qv_bias.reshape(2 * width)])
    bias_all = jnp.stack(
        [own_biases] + [xor_permute(own_biases, "tensor", mask) for mask in range(1, GROUPS)], 0
    ).astype(jnp.float32)
    fc1_bias_all = jnp.transpose(
        xor_order(bias_all[:, :hidden].reshape(GROUPS, 2, 2, 2, part), place, (1, 2, 3)),
        (3, 1, 2, 0, 4),
    ).reshape(GROUPS * hidden)
    qv_all = xor_order(
        bias_all[:, hidden:].reshape(GROUPS, 2, 2, 2, 2, slot), place, (2, 3, 4)
    ).reshape(GROUPS, 2, width)
    qkv_bias = jnp.stack([qv_all[:, 0], jnp.zeros_like(qv_all[:, 0]), qv_all[:, 1]], 1).reshape(
        GROUPS * 3 * width
    )

    modulation, attention_shares = window((modulation, attention_shares), weights)
    attention_all = jnp.stack([jnp.stack(chips, 0) for chips in weights.result], 0)
    qkv_rows = jnp.transpose(
        attention_all[:, :, :, : 3 * slot].reshape(2, 4, GROUPS, 3, slot, model_width),
        (2, 3, 1, 0, 4, 5),
    ).reshape(GROUPS * 3 * width, model_width)
    proj_rows = jnp.transpose(attention_all[:, :, :, 3 * slot :], (2, 1, 0, 3, 4)).reshape(
        GROUPS * width, model_width
    )
    (modulation, qkv_rows, proj_rows, pieces, grad_pieces, fc1_shares, own_fc1, own_fc2) = window(
        (modulation, qkv_rows, proj_rows, pieces, grad_pieces, fc1_shares, own_fc1, own_fc2),
        incoming[0],
    )
    modulation = modulation.astype(jnp.float32)
    shift1, scale1, gate1, shift2, scale2, gate2 = [
        modulation[:, index][:, None] for index in range(6)
    ]
    fc1_flow = Flow(gather_local(own_fc1, fc1_shares, (0, 1, 2)))
    tokens_in, attn_in, qkv, attended, log_totals = [], [], [], [], []
    for index in range(latents):
        tokens_in.append(incoming[index].result.reshape(seq, model_width))
        normed = layer_stats(tokens_in[index].astype(jnp.float32))[0]
        attn_in.append((normed * (1.0 + scale1[index]) + shift1[index]).astype(jnp.bfloat16))
        qkv.append((_nt(attn_in[index], qkv_rows) + qkv_bias).astype(jnp.bfloat16))
        if index == 0:
            qkv[0], pieces = window((qkv[0], pieces), fc1_flow)
            incoming += [Flow(sent(pieces[other], exchange)) for other in range(1, latents)]
        if index == 1:
            qkv[1], grad_pieces = window((qkv[1], grad_pieces), fc1_flow, fc2_flow)
            grad_flows = [Flow(sent(grad_pieces[0], exchange))]
        result, totals = attend(qkv[index], 1, GROUPS, width, seq)
        if index == 0:
            result, own_fc2 = window((result, own_fc2), fc1_flow, *incoming[1:])
            fc2_flow = Flow(gather_local(own_fc2, fc2_shares, (0, 1, 2)))
        if index == 1:
            result, grad_pieces = window((result, grad_pieces), fc1_flow, fc2_flow, *grad_flows)
            grad_flows += [
                Flow(sent(grad_pieces[other], exchange)) for other in range(1, latents)
            ]
        attended.append(result)
        log_totals.append(totals)

    def dense(blocks):
        return jnp.concatenate(
            [block.reshape(-1, model_width) for chips in blocks for block in chips], 0
        )

    fc1_rows = dense(fc1_flow.result)
    attended_all = jnp.concatenate(attended, 0)
    inputs_float = jnp.stack(tokens_in, 0).astype(jnp.float32)
    attn_out = (
        jnp.dot(attended_all, proj_rows, preferred_element_type=jnp.float32)
        + proj_bias.astype(jnp.float32)
    ).reshape(latents, seq, model_width)

    attn_out = window(attn_out, fc2_flow)
    mid = inputs_float + gate1 * attn_out
    norm2, inverse2 = layer_stats(mid)
    mlp_in = (norm2 * (1.0 + scale2) + shift2).astype(jnp.bfloat16).reshape(rows, model_width)
    pre = _nt(mlp_in, fc1_rows) + fc1_bias_all
    act = jax.nn.gelu(pre, approximate=True).astype(jnp.bfloat16)
    act, pre = window((act, pre), fc2_flow, *grad_flows[1:])
    fc2_rows = dense(fc2_flow.result)
    grad_out = jnp.stack(
        [flow.result.reshape(seq, model_width) for flow in grad_flows], 0
    ).astype(jnp.float32)
    mlp_out = (
        jnp.dot(act, fc2_rows, preferred_element_type=jnp.float32) + fc2_bias.astype(jnp.float32)
    ).reshape(latents, seq, model_width)
    out_local = (mid + gate2 * mlp_out).astype(jnp.bfloat16)
    grad_gate2 = jnp.sum(grad_out * mlp_out, 1)
    d_mlp = (grad_out * gate2).astype(jnp.bfloat16).reshape(rows, model_width)
    out_local, grad_gate2, d_mlp = lax.optimization_barrier((out_local, grad_gate2, d_mlp))
    out_pieces = jnp.transpose(
        out_local.reshape(latents, GROUPS, row_count, model_width), (1, 0, 2, 3)
    )
    out_flow = Flow(sent(out_pieces, exchange))
    dense_shape = (2, 4, GROUPS, part, model_width)
    fc2_bias_part = jnp.sum(d_mlp.astype(jnp.float32), 0)
    fc2_local = contract(act, d_mlp).astype(jnp.bfloat16)
    d_mlp, fc2_local = lax.optimization_barrier((d_mlp, fc2_local))
    fc2_sum = Flow(reduce_local(fc2_local.reshape(dense_shape), (0, 1, 2)))
    d_act = _nt(d_mlp, fc2_rows)
    d_pre = jax.vjp(partial(jax.nn.gelu, approximate=True), pre)[1](d_act)[0].astype(jnp.bfloat16)
    d_pre = window(d_pre, fc2_sum)
    fc1_bias_part = jnp.sum(d_pre.astype(jnp.float32), 0)
    fc1_local = contract(d_pre, mlp_in).astype(jnp.bfloat16)
    d_pre, fc1_local = window((d_pre, fc1_local), fc2_sum, out_flow)
    fc1_sum = Flow(reduce_local(fc1_local.reshape(dense_shape), (0, 1, 2)))
    d_mlp_in = jnp.dot(d_pre, fc1_rows, preferred_element_type=jnp.float32).reshape(
        latents, seq, model_width
    )
    d_mlp_in = window(d_mlp_in, fc2_sum, fc1_sum)
    grad_shift2 = jnp.sum(d_mlp_in, 1)
    grad_scale2 = jnp.sum(d_mlp_in * norm2, 1)
    d_mid = grad_out + norm_back(d_mlp_in * (1.0 + scale2), norm2, inverse2)
    grad_gate1 = jnp.sum(d_mid * attn_out, 1)
    d_attn = (d_mid * gate1).astype(jnp.bfloat16).reshape(rows, model_width)
    proj_bias_part = jnp.sum(d_attn.astype(jnp.float32), 0)
    proj_local = contract(attended_all, d_attn).astype(jnp.bfloat16)
    d_attended = _nt(d_attn, proj_rows).astype(jnp.bfloat16)
    d_attended, proj_local = window((d_attended, proj_local), fc2_sum, fc1_sum)
    fc2_rows_flow = Flow(gathered(fc2_sum.result))
    proj_sum = Flow(
        reduce_local(
            jnp.transpose(proj_local.reshape(GROUPS, 4, 2, slot, model_width), (2, 1, 0, 3, 4)),
            (1,),
        )
    )

    fc1_true = xor_order(
        jnp.transpose(fc1_bias_part.reshape(2, 2, 2, GROUPS, part), (3, 1, 2, 0, 4)),
        place,
        (1, 2, 3),
    ).reshape(GROUPS, hidden)
    everywhere = jnp.concatenate([fc2_bias_part, proj_bias_part])

    def sum_biases():
        own = [
            jnp.concatenate([fc1_true[mask], everywhere]).astype(jnp.bfloat16)
            for mask in range(GROUPS)
        ]
        total = yield group_send(own)
        total = group_add(total).astype(jnp.bfloat16)
        pair = yield (total, xor_permute(total, "dp", 1))
        total = add_low(*pair)
        total = add_low(total, xor_permute(total, "dp", 2))
        pair = yield (total, xor_permute(total, "dp", 4))
        return add_low(*pair).astype(jnp.float32)

    biases = Flow(sum_biases())

    d_qkv, grad_shift1, grad_scale1, returned = [], [], [], []
    d_attended = [d_attended[index * seq : (index + 1) * seq] for index in range(latents)]
    qkv_local, qkv_bias_part = 0.0, 0.0
    qkv_sum = None
    for index in range(latents):
        d_qkv.append(
            attend_back(
                qkv[index],
                attended[index],
                log_totals[index],
                d_attended[index],
                1,
                GROUPS,
                width,
                seq,
            )
        )
        last = index == latents - 1
        if index == 0:
            d_qkv[0] = window(d_qkv[0], fc2_rows_flow, fc1_sum, proj_sum, biases)
        if last:
            d_qkv[index] = window(d_qkv[index], later_rows_flow, biases, *returned)
        qkv_bias_part = qkv_bias_part + jnp.sum(d_qkv[index].astype(jnp.float32), 0)
        qkv_local = qkv_local + contract(d_qkv[index], attn_in[index])
        if last:
            qkv_blocks = jnp.transpose(
                qkv_local.astype(jnp.bfloat16).reshape(GROUPS, 3, 4, 2, slot, model_width),
                (3, 2, 0, 1, 4, 5),
            ).reshape(2, 4, GROUPS, 3 * slot, model_width)
            d_qkv[index], qkv_blocks = lax.optimization_barrier((d_qkv[index], qkv_blocks))
            qkv_sum = Flow(reduce_local(qkv_blocks, (0,)))
        d_attn_in = jnp.dot(d_qkv[index], qkv_rows, preferred_element_type=jnp.float32)
        norm1, inverse1 = layer_stats(tokens_in[index].astype(jnp.float32))
        grad_shift1.append(jnp.sum(d_attn_in, 0))
        grad_scale1.append(jnp.sum(d_attn_in * norm1, 0))
        local = d_mid[index] + norm_back(d_attn_in * (1.0 + scale1[index]), norm1, inverse1)
        local = local.astype(jnp.bfloat16).reshape(GROUPS, row_count, model_width)
        if last:
            local = window(local, qkv_sum)
        else:
            flows = (fc1_sum, proj_sum, biases)
            (local, d_attended[index + 1], qkv_local) = window(
                (local, d_attended[index + 1], qkv_local), *(flows if index == 0 else ())
            )
        returned.append(Flow(sent(local, exchange)))
        if index == 0:
            later_rows_flow = Flow(gathered(fc1_sum.result, proj_sum.result))
    window((), qkv_sum, returned[-1])
    qkv_rows_flow = Flow(gathered(qkv_sum.result))
    qkv_rows_flow.advance(qkv_rows_flow.values)
    grad_tokens = merge_latents([flow.result for flow in returned], jnp.float32)
    output = jnp.transpose(out_flow.result, (2, 0, 1, 3)).reshape(
        row_count, group_latents, model_width
    )
    grad_fc2 = fc2_rows_flow.result[0].reshape(hidden, model_width).astype(jnp.float32)
    grad_fc1 = later_rows_flow.result[0].reshape(hidden, model_width).astype(jnp.float32).T
    grad_proj = later_rows_flow.result[1].reshape(width, model_width).astype(jnp.float32)
    grad_qkv = jnp.transpose(
        qkv_rows_flow.result[0].reshape(SHARES, 3, slot, model_width).astype(jnp.float32), (3, 1, 0, 2)
    ).reshape(model_width, 3, width)

    d_modulation = jnp.stack(
        [
            jnp.stack(grad_shift1, 0),
            jnp.stack(grad_scale1, 0),
            grad_gate1,
            grad_shift2,
            grad_scale2,
            grad_gate2,
        ],
        1,
    ).astype(jnp.bfloat16)
    qkv_true = xor_order(
        qkv_bias_part.reshape(GROUPS, 3, 2, 2, 2, slot), place, (2, 3, 4)
    ).reshape(GROUPS, 3 * width)
    d_mod_parts = d_modulation.reshape(latents, 6, GROUPS, width)
    got = group_send(
        [
            jnp.concatenate(
                [
                    lax.dynamic_index_in_dim(d_mod_parts, me ^ mask, 2, keepdims=False).reshape(
                        latents * 6 * width
                    ),
                    qkv_true[mask].astype(jnp.bfloat16),
                ]
            )
            for mask in range(GROUPS)
        ]
    )
    d_mod_group = jnp.stack([piece[: latents * 6 * width] for piece in got], 0).reshape(
        group_latents, 6 * width
    )
    qkv_group = group_add([piece[latents * 6 * width :] for piece in got]).astype(jnp.bfloat16)

    def member_order(array):
        return xor_order(
            array.reshape(2, 2, latents, model_width), me, (0, 1)
        ).reshape(group_latents, model_width)

    everyone = lax.all_gather(
        jnp.concatenate(
            [d_mod_group, member_order(silu_c), qkv_group.reshape(group_latents, -1)], 1
        ),
        "dp",
        axis=0,
    )
    d_mod_all = everyone[:, :, : 6 * width].reshape(-1, 6 * width)
    silu_all = everyone[:, :, 6 * width : 6 * width + model_width].reshape(-1, model_width)
    grad_qv_bias = jnp.sum(
        everyone[:, :, 6 * width + model_width :].reshape(-1, 3, width).astype(jnp.float32), 0
    )[::2]
    grad_ada_bias = jnp.sum(d_mod_all.astype(jnp.float32), 0).reshape(6, width)
    grad_ada = contract(silu_all, d_mod_all).reshape(model_width, 6, width)
    d_silu = member_order(_nt(d_mod_group, ada_flat).astype(jnp.bfloat16))
    d_silu = group_add(group_send([d_silu] * GROUPS))
    grad_cond = jax.vjp(jax.nn.silu, cond_float)[1](d_silu)[0]
    grad_fc1_bias = biases.result[:hidden]
    grad_fc2_bias = biases.result[hidden : hidden + model_width]
    grad_proj_bias = biases.result[hidden + model_width :]
    return (
        output,
        grad_tokens,
        grad_cond,
        grad_qkv,
        grad_qv_bias,
        grad_proj,
        grad_proj_bias,
        grad_fc1,
        grad_fc1_bias,
        grad_fc2,
        grad_fc2_bias,
        grad_ada,
        grad_ada_bias,
    )


def shards(tokens, cond, cotangent, qkv_weight, *rest):
    even = (
        lax.axis_size("tensor") == GROUPS
        and lax.axis_size("dp") == SHARES
        and tokens.shape[1] % GROUPS == 0
        and qkv_weight.shape[2] == 4 * HD
    )
    program = whole_latents if even else split_heads
    return program(tokens, cond, cotangent, qkv_weight, *rest)


def solution(mesh):
    return jax.shard_map(
        shards,
        mesh=mesh,
        in_specs=(
            P("tensor", "dp", None),
            P("dp", None),
            P("tensor", "dp", None),
            P(None, None, "tensor"),
            P(None, "tensor"),
            P("tensor", None),
            P(),
            P(None, "tensor"),
            P("tensor"),
            P("tensor", None),
            P(),
            P(None, None, "tensor"),
            P(None, "tensor"),
        ),
        out_specs=(
            P("tensor", "dp", None),
            P("tensor", "dp", None),
            P("dp", None),
            P(None, None, "tensor"),
            P(None, "tensor"),
            P("tensor", None),
            P(),
            P(None, "tensor"),
            P("tensor"),
            P("tensor", None),
            P(),
            P(None, None, "tensor"),
            P(None, "tensor"),
        ),
        check_vma=False,
    )
```

```python
from functools import partial

import jax
import jax.numpy as jnp
from jax import lax
from jax.experimental import pallas as pl
from jax.experimental.pallas import tpu as pltpu
from jax.sharding import PartitionSpec as P

HD = 64
LANES = 128


def layer_stats(values):
    row_mean = jnp.mean(values, -1, keepdims=True)
    centered = values - row_mean
    variance = jnp.mean(centered * centered, -1, keepdims=True)
    inverse = lax.rsqrt(variance + 1e-06)
    return (centered * inverse, inverse)


def norm_back(d_norm, normed, inverse):
    first = jnp.mean(d_norm, -1, keepdims=True)
    second = jnp.mean(d_norm * normed, -1, keepdims=True)
    return inverse * (d_norm - first - normed * second)


def split_heads(
    tokens,
    cond,
    cotangent,
    qkv_weight,
    qv_bias,
    output_projection_weight,
    proj_bias,
    fc1_weight,
    fc1_bias,
    fc2_weight,
    fc2_bias,
    ada_weight,
    ada_bias,
):
    row_count, latents, model_width = tokens.shape
    local_width = qkv_weight.shape[2]
    heads_local = local_width // HD
    seq_len = row_count * lax.axis_size("tensor")
    factor = HD ** (-0.5)

    def to_heads(array):
        return jnp.transpose(array.reshape(seq_len, latents, heads_local, HD), (1, 2, 0, 3))

    def from_heads(array):
        return jnp.transpose(array, (2, 0, 1, 3)).reshape(seq_len, latents, local_width)

    def attend(block):
        query_blk, key_blk, value_blk = block
        scores = (
            jnp.einsum("hqd,hkd->hqk", query_blk, key_blk, preferred_element_type=jnp.float32)
            * factor
        )
        row_max = jnp.max(scores, -1, keepdims=True)
        log_total = row_max + jnp.log(jnp.sum(jnp.exp(scores - row_max), -1, keepdims=True))
        probs = jnp.exp(scores - log_total).astype(jnp.bfloat16)
        result = jnp.einsum("hqk,hkd->hqd", probs, value_blk, preferred_element_type=jnp.float32)
        return (result.astype(jnp.bfloat16), log_total[..., 0])

    def attend_back(block):
        query_blk, key_blk, value_blk, log_total, grad_blk = block
        scores = (
            jnp.einsum("hqd,hkd->hqk", query_blk, key_blk, preferred_element_type=jnp.float32)
            * factor
        )
        weights = jnp.exp(scores - log_total[..., None])
        d_probs = jnp.einsum(
            "hqd,hkd->hqk", grad_blk, value_blk, preferred_element_type=jnp.float32
        )
        d_scores = (weights * (d_probs - jnp.sum(d_probs * weights, -1, keepdims=True))).astype(
            jnp.bfloat16
        )
        d_query = (
            jnp.einsum("hqk,hkd->hqd", d_scores, key_blk, preferred_element_type=jnp.float32)
            * factor
        ).astype(jnp.bfloat16)
        d_key = (
            jnp.einsum("hqk,hqd->hkd", d_scores, query_blk, preferred_element_type=jnp.float32)
            * factor
        ).astype(jnp.bfloat16)
        d_value = jnp.einsum(
            "hqk,hqd->hkd",
            weights.astype(jnp.bfloat16),
            grad_blk,
            preferred_element_type=jnp.float32,
        ).astype(jnp.bfloat16)
        return (d_query, d_key, d_value)

    cond_float = cond.astype(jnp.float32)
    silu_c = jax.nn.silu(cond_float).astype(jnp.bfloat16)
    ada_flat = ada_weight.reshape(model_width, 6 * local_width)
    mod_part = jnp.dot(silu_c, ada_flat, preferred_element_type=jnp.float32) + ada_bias.reshape(
        6 * local_width
    ).astype(jnp.float32)
    mod_part = mod_part.reshape(latents, 6, local_width).astype(jnp.bfloat16)
    modulation = lax.all_gather(mod_part, "tensor", axis=2, tiled=True).astype(jnp.float32)
    shift1, scale1, gate1, shift2, scale2, gate2 = [
        modulation[:, index][None] for index in range(6)
    ]
    first_dense_weight_gathered, second_dense_weight_gathered, fc1_bias_full = (
        lax.all_gather(fc1_weight, "tensor", axis=1, tiled=True),
        lax.all_gather(fc2_weight, "tensor", axis=0, tiled=True),
        lax.all_gather(fc1_bias, "tensor", axis=0, tiled=True),
    )
    inputs_float = tokens.astype(jnp.float32)
    norm1, inverse1 = layer_stats(inputs_float)
    attn_in = (norm1 * (1.0 + scale1) + shift1).astype(jnp.bfloat16)
    attention_gathered = lax.all_gather(attn_in, "tensor", axis=0, tiled=True)
    query_key_value_rows = qkv_weight.reshape(model_width, 3 * local_width)
    projected = jnp.einsum(
        "rap,po->rao", attention_gathered, query_key_value_rows, preferred_element_type=jnp.float32
    ).reshape(seq_len, latents, 3, local_width)
    bias_float = qv_bias.astype(jnp.float32)
    queries = to_heads((projected[:, :, 0] + bias_float[0]).astype(jnp.bfloat16))
    keys_all = to_heads(projected[:, :, 1].astype(jnp.bfloat16))
    values_all = to_heads((projected[:, :, 2] + bias_float[1]).astype(jnp.bfloat16))
    attended_heads, log_totals = lax.map(attend, (queries, keys_all, values_all))
    attention_result = from_heads(attended_heads)
    shard_slice = attention_result
    attn_out = lax.psum_scatter(
        jnp.einsum(
            "pac,cx->pax", shard_slice, output_projection_weight, preferred_element_type=jnp.float32
        ).astype(jnp.bfloat16),
        "tensor",
        scatter_dimension=0,
        tiled=True,
    ).astype(jnp.float32) + proj_bias.astype(jnp.float32)
    mid = inputs_float + gate1 * attn_out
    norm2, inverse2 = layer_stats(mid)
    feedforward_input = (norm2 * (1.0 + scale2) + shift2).astype(jnp.bfloat16)
    pre = jnp.einsum(
        "biw,wr->bir",
        feedforward_input,
        first_dense_weight_gathered,
        preferred_element_type=jnp.float32,
    ) + fc1_bias_full.astype(jnp.float32)
    gelu_activation = jax.nn.gelu(pre, approximate=True).astype(jnp.bfloat16)
    mlp_out = jnp.einsum(
        "gzw,wt->gzt",
        gelu_activation,
        second_dense_weight_gathered,
        preferred_element_type=jnp.float32,
    ) + fc2_bias.astype(jnp.float32)
    output = (mid + gate2 * mlp_out).astype(jnp.bfloat16)
    grad_out = cotangent.astype(jnp.float32)
    grad_gate2 = jnp.sum(grad_out * mlp_out, 0)
    feedforward_gradient = (grad_out * gate2).astype(jnp.bfloat16)
    fc2_bias_part = jnp.sum(feedforward_gradient.astype(jnp.float32), (0, 1))
    second_dense_gradient_shard = jnp.einsum(
        "rqu,rqf->uf", gelu_activation, feedforward_gradient, preferred_element_type=jnp.float32
    )
    activation_gradient = jnp.einsum(
        "zqy,vy->zqv",
        feedforward_gradient,
        second_dense_weight_gathered,
        preferred_element_type=jnp.float32,
    )
    gelu_pull = jax.vjp(partial(jax.nn.gelu, approximate=True), pre)[1]
    preactivation_gradient = gelu_pull(activation_gradient)[0].astype(jnp.bfloat16)
    fc1_bias_part = jnp.sum(preactivation_gradient.astype(jnp.float32), (0, 1))
    first_dense_gradient_shard = jnp.einsum(
        "hic,hip->cp", feedforward_input, preactivation_gradient, preferred_element_type=jnp.float32
    )
    feedforward_input_gradient = jnp.einsum(
        "xfg,yg->xfy",
        preactivation_gradient,
        first_dense_weight_gathered,
        preferred_element_type=jnp.float32,
    )
    grad_fc1, grad_fc2, grad_fc1_bias = (
        lax.psum_scatter(
            first_dense_gradient_shard.astype(jnp.bfloat16),
            "tensor",
            scatter_dimension=1,
            tiled=True,
        ).astype(jnp.float32),
        lax.psum_scatter(
            second_dense_gradient_shard.astype(jnp.bfloat16),
            "tensor",
            scatter_dimension=0,
            tiled=True,
        ).astype(jnp.float32),
        lax.psum_scatter(
            fc1_bias_part.astype(jnp.bfloat16), "tensor", scatter_dimension=0, tiled=True
        ).astype(jnp.float32),
    )
    grad_shift2 = jnp.sum(feedforward_input_gradient, 0)
    grad_scale2 = jnp.sum(feedforward_input_gradient * norm2, 0)
    d_mid = grad_out + norm_back(feedforward_input_gradient * (1.0 + scale2), norm2, inverse2)
    grad_gate1 = jnp.sum(d_mid * attn_out, 0)
    d_attn = (d_mid * gate1).astype(jnp.bfloat16)
    proj_bias_part = jnp.sum(d_attn.astype(jnp.float32), (0, 1))
    attention_gathered_gradient = lax.all_gather(d_attn, "tensor", axis=0, tiled=True)
    output_projection_gradient = jnp.einsum(
        "pti,ptq->iq",
        attention_result,
        attention_gathered_gradient,
        preferred_element_type=jnp.float32,
    )
    d_attended = jnp.einsum(
        "btw,vw->btv",
        attention_gathered_gradient,
        output_projection_weight,
        preferred_element_type=jnp.float32,
    ).astype(jnp.bfloat16)
    d_query_h, d_key_h, d_value_h = lax.map(
        attend_back, (queries, keys_all, values_all, log_totals, to_heads(d_attended))
    )
    d_queries = from_heads(d_query_h)
    d_values = from_heads(d_value_h)
    query_key_value_gradient = jnp.stack([d_queries, from_heads(d_key_h), d_values], 2).reshape(
        seq_len, latents, 3 * local_width
    )
    grad_qv_bias = jnp.stack(
        [
            jnp.sum(d_queries.astype(jnp.float32), (0, 1)),
            jnp.sum(d_values.astype(jnp.float32), (0, 1)),
        ],
        0,
    )
    grad_qkv = jnp.einsum(
        "iyz,iyn->zn",
        attention_gathered,
        query_key_value_gradient,
        preferred_element_type=jnp.float32,
    ).reshape(model_width, 3, local_width)
    shard_slice = query_key_value_gradient
    d_attn_in = lax.psum_scatter(
        jnp.einsum(
            "rnt,mt->rnm", shard_slice, query_key_value_rows, preferred_element_type=jnp.float32
        ).astype(jnp.bfloat16),
        "tensor",
        scatter_dimension=0,
        tiled=True,
    ).astype(jnp.float32)
    grad_shift1 = jnp.sum(d_attn_in, 0)
    grad_scale1 = jnp.sum(d_attn_in * norm1, 0)
    grad_tokens = d_mid + norm_back(d_attn_in * (1.0 + scale1), norm1, inverse1)
    d_modulation = jnp.stack(
        [grad_shift1, grad_scale1, grad_gate1, grad_shift2, grad_scale2, grad_gate2], 1
    )
    d_mod_local = lax.psum_scatter(
        d_modulation.astype(jnp.bfloat16), "tensor", scatter_dimension=2, tiled=True
    ).astype(jnp.float32)
    grad_ada_bias = jnp.sum(d_mod_local, 0)
    d_mod_flat = d_mod_local.reshape(latents, 6 * local_width)
    grad_ada = jnp.dot(
        silu_c.astype(jnp.float32).T, d_mod_flat, precision=lax.Precision.HIGHEST
    ).reshape(model_width, 6, local_width)
    d_silu_part = jnp.dot(
        d_mod_flat, ada_flat.astype(jnp.float32).T, precision=lax.Precision.HIGHEST
    )
    d_silu, grad_fc2_bias, grad_proj_bias = (
        lax.psum(d_silu_part.astype(jnp.bfloat16), "tensor").astype(jnp.float32),
        lax.psum(fc2_bias_part.astype(jnp.bfloat16), "tensor").astype(jnp.float32),
        lax.psum(proj_bias_part.astype(jnp.bfloat16), "tensor").astype(jnp.float32),
    )
    silu_pull = jax.vjp(jax.nn.silu, cond_float)[1]
    grad_cond = silu_pull(d_silu)[0]
    (
        grad_qkv,
        grad_qv_bias,
        output_projection_gradient,
        grad_proj_bias,
        grad_fc1,
        grad_fc1_bias,
        grad_fc2,
        grad_fc2_bias,
        grad_ada,
        grad_ada_bias,
    ) = (
        lax.psum(grad_qkv.astype(jnp.bfloat16), "dp").astype(jnp.float32),
        lax.psum(grad_qv_bias.astype(jnp.bfloat16), "dp").astype(jnp.float32),
        lax.psum(output_projection_gradient.astype(jnp.bfloat16), "dp").astype(jnp.float32),
        lax.psum(grad_proj_bias.astype(jnp.bfloat16), "dp").astype(jnp.float32),
        lax.psum(grad_fc1.astype(jnp.bfloat16), "dp").astype(jnp.float32),
        lax.psum(grad_fc1_bias.astype(jnp.bfloat16), "dp").astype(jnp.float32),
        lax.psum(grad_fc2.astype(jnp.bfloat16), "dp").astype(jnp.float32),
        lax.psum(grad_fc2_bias.astype(jnp.bfloat16), "dp").astype(jnp.float32),
        lax.psum(grad_ada.astype(jnp.bfloat16), "dp").astype(jnp.float32),
        lax.psum(grad_ada_bias.astype(jnp.bfloat16), "dp").astype(jnp.float32),
    )
    return (
        output,
        grad_tokens,
        grad_cond,
        grad_qkv,
        grad_qv_bias,
        output_projection_gradient,
        grad_proj_bias,
        grad_fc1,
        grad_fc1_bias,
        grad_fc2,
        grad_fc2_bias,
        grad_ada,
        grad_ada_bias,
    )


def _nt(left, right):
    return lax.dot_general(
        left, right, (((1,), (1,)), ((), ())), preferred_element_type=jnp.float32
    )


def _attend_kernel(qkv_ref, out_ref, lse_ref, *, width, rows):
    lane = lax.broadcasted_iota(jnp.int32, (1, LANES), 1)
    first = lane < HD

    def chunk(index, carry):
        at = pl.ds(pl.multiple_of(index * rows, rows), rows)
        totals = jnp.zeros((rows, LANES), jnp.float32)
        for pair in range(width // LANES):
            lo = pair * LANES
            query = qkv_ref[at, lo : lo + LANES] * jnp.bfloat16(HD**-0.5)
            key = qkv_ref[:, width + lo : width + lo + LANES]
            value = qkv_ref[:, 2 * width + lo : 2 * width + lo + LANES]
            parts = []
            for side in range(2):
                mine = first if side == 0 else jnp.logical_not(first)
                scores = _nt(jnp.where(mine, query, 0), key)
                top = jnp.max(scores, -1, keepdims=True)
                weights = jnp.exp(scores - top).astype(jnp.bfloat16)
                mixed = jnp.dot(
                    weights, jnp.where(mine, value, 1), preferred_element_type=jnp.float32
                )
                other = HD * (1 - side)
                total = mixed[:, other : other + 1]
                parts.append(mixed / total)
                totals = jnp.where(lane == 2 * pair + side, top + jnp.log(total), totals)
            out_ref[at, lo : lo + LANES] = jnp.where(first, parts[0], parts[1]).astype(
                jnp.bfloat16
            )
        lse_ref[at, :] = totals
        return carry

    lax.fori_loop(0, qkv_ref.shape[0] // rows, chunk, 0)


def attend(qkv, latents, groups, width, seq):
    heads = groups * (width // HD)
    work = latents * heads * seq * seq
    return pl.pallas_call(
        partial(_attend_kernel, width=width, rows=min(256, seq)),
        grid=(latents, groups),
        in_specs=[pl.BlockSpec((seq, 3 * width), lambda i, j: (i, j))],
        out_specs=[
            pl.BlockSpec((seq, width), lambda i, j: (i, j)),
            pl.BlockSpec((seq, LANES), lambda i, j: (i, j)),
        ],
        out_shape=[
            jax.ShapeDtypeStruct((latents * seq, groups * width), jnp.bfloat16),
            jax.ShapeDtypeStruct((latents * seq, groups * LANES), jnp.float32),
        ],
        compiler_params=pltpu.CompilerParams(vmem_limit_bytes=40 * 2**20),
        cost_estimate=pl.CostEstimate(
            flops=16 * HD * work,
            bytes_accessed=latents * seq * groups * (8 * width + 4 * LANES),
            transcendentals=work,
        ),
        name="attend",
    )(qkv)


def _split3(column):
    high = column.astype(jnp.bfloat16).astype(jnp.float32)
    middle = (column - high).astype(jnp.bfloat16).astype(jnp.float32)
    return (high, middle, column - high - middle)


def _attend_back_kernel(qkv_ref, out_ref, lse_ref, grad_ref, dqkv_ref, *, width, rows):
    seq = qkv_ref.shape[0]
    lane = lax.broadcasted_iota(jnp.int32, (1, LANES), 1)
    first = lane < HD
    scale = jnp.bfloat16(HD**-0.5)

    def extend(mine, base, array, column):
        high, middle, low = _split3(column)
        extra = jnp.where(
            lane == base,
            high,
            jnp.where(lane == base + 1, middle, jnp.where(lane == base + 2, low, 0.0)),
        )
        return jnp.where(mine, array, extra.astype(jnp.bfloat16))

    for pair in range(width // LANES):
        lo = pair * LANES
        query = qkv_ref[:, lo : lo + LANES] * scale
        grad = grad_ref[:, lo : lo + LANES]
        product = grad.astype(jnp.float32) * out_ref[:, lo : lo + LANES].astype(jnp.float32)
        queries, grads = [], []
        for side in range(2):
            mine = first if side == 0 else jnp.logical_not(first)
            base = HD * (1 - side)
            head = 2 * pair + side
            queries.append(extend(mine, base, query, -lse_ref[:, head : head + 1]))
            inner = jnp.sum(jnp.where(mine, product, 0.0), -1, keepdims=True)
            grads.append(extend(mine, base, grad, -inner))
        d_query = [jnp.zeros((HD, seq), jnp.float32)] * 2
        for index in range(seq // rows):
            at = slice(index * rows, (index + 1) * rows)
            key = qkv_ref[at, width + lo : width + lo + LANES]
            value = qkv_ref[at, 2 * width + lo : 2 * width + lo + LANES]
            key_t = key.T
            d_key, d_value = [], []
            for side in range(2):
                mine = first if side == 0 else jnp.logical_not(first)
                base = HD * (1 - side)
                ones = jnp.where((lane >= base) & (lane < base + 3), 1.0, 0.0).astype(jnp.bfloat16)
                weights = jnp.exp(_nt(jnp.where(mine, key, ones), queries[side]))
                d_scores = (
                    weights * _nt(jnp.where(mine, value, ones), grads[side])
                ).astype(jnp.bfloat16)
                d_value.append(
                    jnp.dot(
                        weights.astype(jnp.bfloat16), grad, preferred_element_type=jnp.float32
                    )
                )
                d_key.append(jnp.dot(d_scores, query, preferred_element_type=jnp.float32))
                d_query[side] = d_query[side] + jnp.dot(
                    key_t[side * HD : (side + 1) * HD],
                    d_scores,
                    preferred_element_type=jnp.float32,
                )
            dqkv_ref[at, width + lo : width + lo + LANES] = jnp.where(
                first, d_key[0], d_key[1]
            ).astype(jnp.bfloat16)
            dqkv_ref[at, 2 * width + lo : 2 * width + lo + LANES] = jnp.where(
                first, d_value[0], d_value[1]
            ).astype(jnp.bfloat16)
        d_query_t = jnp.concatenate(d_query, 0) * (HD**-0.5)
        dqkv_ref[:, lo : lo + LANES] = d_query_t.T.astype(jnp.bfloat16)


def attend_back(qkv, out, lse, grad, latents, groups, width, seq):
    heads = groups * (width // HD)
    work = latents * heads * seq * seq
    return pl.pallas_call(
        partial(_attend_back_kernel, width=width, rows=min(256, seq)),
        grid=(latents, groups),
        in_specs=[
            pl.BlockSpec((seq, 3 * width), lambda i, j: (i, j)),
            pl.BlockSpec((seq, width), lambda i, j: (i, j)),
            pl.BlockSpec((seq, LANES), lambda i, j: (i, j)),
            pl.BlockSpec((seq, width), lambda i, j: (i, j)),
        ],
        out_specs=pl.BlockSpec((seq, 3 * width), lambda i, j: (i, j)),
        out_shape=jax.ShapeDtypeStruct(qkv.shape, jnp.bfloat16),
        compiler_params=pltpu.CompilerParams(vmem_limit_bytes=48 * 2**20),
        cost_estimate=pl.CostEstimate(
            flops=40 * HD * work,
            bytes_accessed=latents * seq * groups * (16 * width + 4 * LANES),
            transcendentals=work,
        ),
        name="attend_back",
    )(qkv, out, lse, grad)


SHARES, GROUPS = 8, 4


def xor_permute(array, axis, mask):
    size = lax.axis_size(axis)
    return lax.ppermute(array, axis, [(index, index ^ mask) for index in range(size)])


def xor_order(array, index, axes):
    for place, axis in enumerate(reversed(axes)):
        array = jnp.where((index >> place) & 1 == 1, jnp.flip(array, axis), array)
    return array


def add_low(left, right):
    return (left.astype(jnp.float32) + right.astype(jnp.float32)).astype(jnp.bfloat16)


def _split_kernel(array_ref, *piece_refs):
    by_latent = jnp.swapaxes(array_ref[...].astype(jnp.float32), 0, 1).astype(jnp.bfloat16)
    latents = len(piece_refs)
    for index, piece_ref in enumerate(piece_refs):
        for member in range(GROUPS):
            piece_ref[member] = by_latent[member * latents + index]


def split_latents(array, latents):
    count, _, depth = array.shape
    step = 32
    return pl.pallas_call(
        _split_kernel,
        grid=(count // step,),
        in_specs=[pl.BlockSpec((step, GROUPS * latents, depth), lambda i: (i, 0, 0))],
        out_specs=[pl.BlockSpec((GROUPS, step, depth), lambda i: (0, i, 0))] * latents,
        out_shape=[jax.ShapeDtypeStruct((GROUPS, count, depth), jnp.bfloat16)] * latents,
        cost_estimate=pl.CostEstimate(flops=0, bytes_accessed=4 * array.size, transcendentals=0),
        name="split_latents",
    )(array)


def _merge_kernel(*refs):
    *piece_refs, array_ref = refs
    pieces = [ref[member] for member in range(GROUPS) for ref in piece_refs]
    array_ref[...] = jnp.swapaxes(
        jnp.stack([piece.astype(jnp.float32) for piece in pieces], 0), 0, 1
    ).astype(array_ref.dtype)


def merge_latents(pieces, dtype):
    _, count, depth = pieces[0].shape
    step, latents = 32, len(pieces)
    size = GROUPS * latents * count * depth
    return pl.pallas_call(
        _merge_kernel,
        grid=(count // step,),
        in_specs=[pl.BlockSpec((GROUPS, step, depth), lambda i: (0, i, 0))] * latents,
        out_specs=pl.BlockSpec((step, GROUPS * latents, depth), lambda i: (i, 0, 0)),
        out_shape=jax.ShapeDtypeStruct((count, GROUPS * latents, depth), dtype),
        cost_estimate=pl.CostEstimate(flops=0, bytes_accessed=6 * size, transcendentals=0),
        name="merge_latents",
    )(*pieces)


class Flow:
    def __init__(self, stages):
        self.stages, self.result = stages, None
        self.values = next(stages)

    def advance(self, values):
        try:
            self.values = self.stages.send(values)
        except StopIteration as stop:
            self.values, self.result = (), stop.value


def window(compute, *flows):
    compute, values = lax.optimization_barrier((compute, [flow.values for flow in flows]))
    for flow, value in zip(flows, values):
        flow.advance(value)
    return compute


def sent(array, move):
    array = yield move(array)
    return array


def gather_local(mine, shares, pauses, direct=False):
    place = lax.axis_index("dp")
    near, far = xor_permute(mine, "tensor", 1), xor_permute(mine, "tensor", 2)
    if direct:
        got = (near, far, xor_permute(mine, "tensor", 3))
    else:
        got = (near, far, xor_permute(far, "tensor", 1))
    if 0 in pauses:
        got = yield got
    block = jnp.stack(got, 0)
    half = mine.shape[0] // 2
    along_x, along_y = xor_permute(block, "dp", 2), xor_permute(block, "dp", 4)
    other = xor_permute(block, "dp", 1)
    if 1 in pauses:
        block, along_x, along_y, other = yield (block, along_x, along_y, other)
    halves = [xor_permute(along_x[:, :half], "dp", 4), xor_permute(along_y[:, half:], "dp", 2)]
    others = [other, xor_permute(along_x, "dp", 1), xor_permute(along_y, "dp", 1)]
    if 2 in pauses:
        halves, others = yield (halves, others)
    across = jnp.concatenate(halves, 1)
    chips = [block, along_x, along_y, across]
    blocks = yield [chips, [*others, xor_permute(across, "dp", 1)]]
    return [
        [
            jnp.concatenate(
                [
                    lax.dynamic_index_in_dim(shares, place ^ (2 * chip + core), 0),
                    blocks[core][chip],
                ],
                0,
            )
            for chip in range(4)
        ]
        for core in range(2)
    ]


def reduce_local(blocks, pauses):
    half = blocks.shape[3] // 2
    pair = (blocks[0], xor_permute(blocks[1], "dp", 1))
    if 0 in pauses:
        pair = yield pair
    total = add_low(*pair)
    total = total.reshape(2, 2, *total.shape[1:])
    first, second = total[:, :, :, :half], total[:, :, :, half:]
    pairs = (
        (first[:, 0], xor_permute(first[:, 1], "dp", 2)),
        (second[0], xor_permute(second[1], "dp", 4)),
    )
    if 1 in pauses:
        pairs = yield pairs
    first, second = [add_low(*pair) for pair in pairs]
    pairs = (
        (first[0], xor_permute(first[1], "dp", 4)),
        (second[0], xor_permute(second[1], "dp", 2)),
    )
    if 2 in pauses:
        pairs = yield pairs
    total = jnp.concatenate([add_low(*pair) for pair in pairs], 1)
    total = total.reshape(2, 2, *total.shape[1:])
    total = add_low(total[:, 0], xor_permute(total[:, 1], "tensor", 1))
    pair = (total[0], xor_permute(total[1], "tensor", 2))
    pair = yield pair
    return add_low(*pair)


def gathered(*shares):
    sizes = [share.shape[0] for share in shares]
    share = jnp.concatenate(shares, 0) if len(shares) > 1 else shares[0]
    whole = yield lax.all_gather(share, "dp", axis=0)
    parts, at = [], 0
    for size in sizes:
        parts.append(whole[:, at : at + size])
        at += size
    return parts


def group_send(pieces):
    return [pieces[0]] + [xor_permute(pieces[mask], "tensor", mask) for mask in range(1, GROUPS)]


def group_add(pieces):
    first, second, third, fourth = [piece.astype(jnp.float32) for piece in pieces]
    return (first + second) + (third + fourth)


def whole_latents(
    tokens,
    cond,
    cotangent,
    qkv_weight,
    qv_bias,
    output_projection_weight,
    proj_bias,
    fc1_weight,
    fc1_bias,
    fc2_weight,
    fc2_bias,
    ada_weight,
    ada_bias,
):
    row_count, group_latents, model_width = tokens.shape
    latents = group_latents // GROUPS
    seq = row_count * GROUPS
    width = qkv_weight.shape[2]
    hidden = fc1_weight.shape[1]
    rows = latents * seq
    part, slot = hidden // SHARES, width // SHARES
    me, place = lax.axis_index("tensor"), lax.axis_index("dp")

    def split_tokens(array):
        return split_latents(array, latents)

    def exchange(pieces):
        return lax.all_to_all(pieces, "tensor", 0, 0)

    def contract(left, right):
        return lax.dot_general(
            left, right, (((0,), (0,)), ((), ())), preferred_element_type=jnp.float32
        )

    qkv_t = jnp.transpose(qkv_weight.reshape(model_width, 3, SHARES, slot), (2, 1, 3, 0))
    attention_shares = jnp.concatenate(
        [
            qkv_t.reshape(SHARES, 3 * slot, model_width),
            output_projection_weight.reshape(SHARES, slot, model_width),
        ],
        1,
    )
    own_qkv = lax.dynamic_index_in_dim(
        qkv_weight.reshape(model_width, 3, SHARES, slot), place, 2, keepdims=False
    )
    own_attention = jnp.concatenate(
        [
            jnp.transpose(own_qkv, (1, 2, 0)).reshape(3 * slot, model_width),
            lax.dynamic_slice_in_dim(output_projection_weight, place * slot, slot, 0),
        ],
        0,
    )
    weights = Flow(gather_local(own_attention, attention_shares, (0,), True))
    cond_float = cond.astype(jnp.float32)
    silu_c = jax.nn.silu(cond_float).astype(jnp.bfloat16)
    ada_flat = ada_weight.reshape(model_width, 6 * width)
    mod_part = jnp.dot(silu_c, ada_flat, preferred_element_type=jnp.float32) + ada_bias.reshape(
        6 * width
    ).astype(jnp.float32)
    mod_part = mod_part.astype(jnp.bfloat16).reshape(GROUPS, latents, 6, width)
    mod_got = []
    for mask in range(GROUPS):
        piece = lax.dynamic_index_in_dim(mod_part, me ^ mask, 0, keepdims=False)
        mod_got.append(xor_permute(piece, "tensor", mask) if mask else piece)
    pieces, mod_got, cotangent, fc1_weight, fc2_weight = window(
        (split_tokens(tokens), mod_got, cotangent, fc1_weight, fc2_weight), weights
    )
    incoming = [Flow(sent(pieces[0], exchange))]
    grad_pieces = split_tokens(cotangent)
    fc1_shares = fc1_weight.T.reshape(SHARES, part, model_width)
    fc2_shares = fc2_weight.reshape(SHARES, part, model_width)
    own_fc1 = lax.dynamic_index_in_dim(fc1_shares, place, 0, keepdims=False)
    own_fc2 = lax.dynamic_index_in_dim(fc2_shares, place, 0, keepdims=False)

    modulation = xor_order(jnp.stack(mod_got, 0).reshape(2, 2, latents, 6, width), me, (0, 1))
    modulation = jnp.transpose(
        modulation.reshape(GROUPS, latents, 6, width), (1, 2, 0, 3)
    ).reshape(latents, 6, model_width)
    own_biases = jnp.concatenate([fc1_bias, qv_bias.reshape(2 * width)])
    bias_all = jnp.stack(
        [own_biases] + [xor_permute(own_biases, "tensor", mask) for mask in range(1, GROUPS)], 0
    ).astype(jnp.float32)
    fc1_bias_all = jnp.transpose(
        xor_order(bias_all[:, :hidden].reshape(GROUPS, 2, 2, 2, part), place, (1, 2, 3)),
        (3, 1, 2, 0, 4),
    ).reshape(GROUPS * hidden)
    qv_all = xor_order(
        bias_all[:, hidden:].reshape(GROUPS, 2, 2, 2, 2, slot), place, (2, 3, 4)
    ).reshape(GROUPS, 2, width)
    qkv_bias = jnp.stack([qv_all[:, 0], jnp.zeros_like(qv_all[:, 0]), qv_all[:, 1]], 1).reshape(
        GROUPS * 3 * width
    )

    (modulation, attention_shares, grad_pieces, fc1_shares, own_fc1) = window(
        (modulation, attention_shares, grad_pieces, fc1_shares, own_fc1), weights
    )
    fc1_flow = Flow(gather_local(own_fc1, fc1_shares, (0, 1, 2)))
    attention_all = jnp.stack([jnp.stack(chips, 0) for chips in weights.result], 0)
    qkv_rows = jnp.transpose(
        attention_all[:, :, :, : 3 * slot].reshape(2, 4, GROUPS, 3, slot, model_width),
        (2, 3, 1, 0, 4, 5),
    ).reshape(GROUPS * 3 * width, model_width)
    proj_rows = jnp.transpose(attention_all[:, :, :, 3 * slot :], (2, 1, 0, 3, 4)).reshape(
        GROUPS * width, model_width
    )
    (modulation, qkv_rows, proj_rows, pieces, grad_pieces, own_fc2) = window(
        (modulation, qkv_rows, proj_rows, pieces, grad_pieces, own_fc2), incoming[0]
    )
    modulation = modulation.astype(jnp.float32)
    shift1, scale1, gate1, shift2, scale2, gate2 = [
        modulation[:, index][:, None] for index in range(6)
    ]
    tokens_in, attn_in, qkv, attended, log_totals = [], [], [], [], []
    for index in range(latents):
        tokens_in.append(incoming[index].result.reshape(seq, model_width))
        normed = layer_stats(tokens_in[index].astype(jnp.float32))[0]
        attn_in.append((normed * (1.0 + scale1[index]) + shift1[index]).astype(jnp.bfloat16))
        qkv.append((_nt(attn_in[index], qkv_rows) + qkv_bias).astype(jnp.bfloat16))
        if index == 0:
            qkv[0], pieces = window((qkv[0], pieces), fc1_flow)
            incoming += [Flow(sent(pieces[other], exchange)) for other in range(1, latents)]
        if index == 1:
            qkv[1], grad_pieces = window((qkv[1], grad_pieces), fc1_flow, fc2_flow)
            grad_flows = [Flow(sent(grad_pieces[0], exchange))]
        result, totals = attend(qkv[index], 1, GROUPS, width, seq)
        if index == 0:
            result, own_fc2 = window((result, own_fc2), fc1_flow, *incoming[1:])
            fc2_flow = Flow(gather_local(own_fc2, fc2_shares, (0, 1, 2)))
        if index == 1:
            result, grad_pieces = window((result, grad_pieces), fc1_flow, fc2_flow, *grad_flows)
            grad_flows += [
                Flow(sent(grad_pieces[other], exchange)) for other in range(1, latents)
            ]
        attended.append(result)
        log_totals.append(totals)

    def dense(blocks):
        return jnp.concatenate(
            [block.reshape(-1, model_width) for chips in blocks for block in chips], 0
        )

    fc1_rows = dense(fc1_flow.result)
    attended_all = jnp.concatenate(attended, 0)
    inputs_float = jnp.stack(tokens_in, 0).astype(jnp.float32)
    attn_out = (
        jnp.dot(attended_all, proj_rows, preferred_element_type=jnp.float32)
        + proj_bias.astype(jnp.float32)
    ).reshape(latents, seq, model_width)

    attn_out = window(attn_out, fc2_flow)
    mid = inputs_float + gate1 * attn_out
    norm2, inverse2 = layer_stats(mid)
    mlp_in = (norm2 * (1.0 + scale2) + shift2).astype(jnp.bfloat16).reshape(rows, model_width)
    pre = _nt(mlp_in, fc1_rows) + fc1_bias_all
    act = jax.nn.gelu(pre, approximate=True).astype(jnp.bfloat16)
    act, pre = window((act, pre), fc2_flow, *grad_flows[1:])
    fc2_rows = dense(fc2_flow.result)
    grad_out = jnp.stack(
        [flow.result.reshape(seq, model_width) for flow in grad_flows], 0
    ).astype(jnp.float32)
    mlp_out = (
        jnp.dot(act, fc2_rows, preferred_element_type=jnp.float32) + fc2_bias.astype(jnp.float32)
    ).reshape(latents, seq, model_width)
    out_local = (mid + gate2 * mlp_out).astype(jnp.bfloat16)
    grad_gate2 = jnp.sum(grad_out * mlp_out, 1)
    d_mlp = (grad_out * gate2).astype(jnp.bfloat16).reshape(rows, model_width)
    out_local, grad_gate2, d_mlp = lax.optimization_barrier((out_local, grad_gate2, d_mlp))
    out_pieces = jnp.transpose(
        out_local.reshape(latents, GROUPS, row_count, model_width), (1, 0, 2, 3)
    )
    out_flow = Flow(sent(out_pieces, exchange))
    dense_shape = (2, 4, GROUPS, part, model_width)
    fc2_bias_part = jnp.sum(d_mlp.astype(jnp.float32), 0)
    fc2_local = contract(act, d_mlp).astype(jnp.bfloat16)
    d_mlp, fc2_local = lax.optimization_barrier((d_mlp, fc2_local))
    fc2_sum = Flow(reduce_local(fc2_local.reshape(dense_shape), (0, 1, 2)))
    d_act = _nt(d_mlp, fc2_rows)
    d_pre = jax.vjp(partial(jax.nn.gelu, approximate=True), pre)[1](d_act)[0].astype(jnp.bfloat16)
    d_pre = window(d_pre, fc2_sum)
    fc1_bias_part = jnp.sum(d_pre.astype(jnp.float32), 0)
    fc1_local = contract(d_pre, mlp_in).astype(jnp.bfloat16)
    d_pre, fc1_local = window((d_pre, fc1_local), fc2_sum, out_flow)
    fc1_sum = Flow(reduce_local(fc1_local.reshape(dense_shape), (0, 1, 2)))
    d_mlp_in = jnp.dot(d_pre, fc1_rows, preferred_element_type=jnp.float32).reshape(
        latents, seq, model_width
    )
    d_mlp_in = window(d_mlp_in, fc2_sum, fc1_sum)
    grad_shift2 = jnp.sum(d_mlp_in, 1)
    grad_scale2 = jnp.sum(d_mlp_in * norm2, 1)
    d_mid = grad_out + norm_back(d_mlp_in * (1.0 + scale2), norm2, inverse2)
    grad_gate1 = jnp.sum(d_mid * attn_out, 1)
    d_attn = (d_mid * gate1).astype(jnp.bfloat16).reshape(rows, model_width)
    proj_bias_part = jnp.sum(d_attn.astype(jnp.float32), 0)
    proj_local = contract(attended_all, d_attn).astype(jnp.bfloat16)
    d_attended = _nt(d_attn, proj_rows).astype(jnp.bfloat16)
    d_attended, proj_local = window((d_attended, proj_local), fc2_sum, fc1_sum)
    fc2_rows_flow = Flow(gathered(fc2_sum.result))
    proj_sum = Flow(
        reduce_local(
            jnp.transpose(proj_local.reshape(GROUPS, 4, 2, slot, model_width), (2, 1, 0, 3, 4)),
            (1,),
        )
    )

    fc1_true = xor_order(
        jnp.transpose(fc1_bias_part.reshape(2, 2, 2, GROUPS, part), (3, 1, 2, 0, 4)),
        place,
        (1, 2, 3),
    ).reshape(GROUPS, hidden)
    everywhere = jnp.concatenate([fc2_bias_part, proj_bias_part])

    def sum_biases():
        own = [
            jnp.concatenate([fc1_true[mask], everywhere]).astype(jnp.bfloat16)
            for mask in range(GROUPS)
        ]
        total = yield group_send(own)
        total = group_add(total).astype(jnp.bfloat16)
        pair = yield (total, xor_permute(total, "dp", 1))
        total = add_low(*pair)
        total = add_low(total, xor_permute(total, "dp", 2))
        pair = yield (total, xor_permute(total, "dp", 4))
        return add_low(*pair).astype(jnp.float32)

    biases = Flow(sum_biases())

    d_qkv, grad_shift1, grad_scale1, returned = [], [], [], []
    d_attended = [d_attended[index * seq : (index + 1) * seq] for index in range(latents)]
    qkv_local, qkv_bias_part = 0.0, 0.0
    qkv_sum = None
    for index in range(latents):
        d_qkv.append(
            attend_back(
                qkv[index],
                attended[index],
                log_totals[index],
                d_attended[index],
                1,
                GROUPS,
                width,
                seq,
            )
        )
        last = index == latents - 1
        if index == 0:
            d_qkv[0] = window(d_qkv[0], fc2_rows_flow, fc1_sum, proj_sum, biases)
        if last:
            d_qkv[index] = window(d_qkv[index], later_rows_flow, biases, *returned)
        qkv_bias_part = qkv_bias_part + jnp.sum(d_qkv[index].astype(jnp.float32), 0)
        qkv_local = qkv_local + contract(d_qkv[index], attn_in[index])
        if last:
            qkv_blocks = jnp.transpose(
                qkv_local.astype(jnp.bfloat16).reshape(GROUPS, 3, 4, 2, slot, model_width),
                (3, 2, 0, 1, 4, 5),
            ).reshape(2, 4, GROUPS, 3 * slot, model_width)
            d_qkv[index], qkv_blocks = lax.optimization_barrier((d_qkv[index], qkv_blocks))
            qkv_sum = Flow(reduce_local(qkv_blocks, (0, 1, 2)))
        d_attn_in = jnp.dot(d_qkv[index], qkv_rows, preferred_element_type=jnp.float32)
        if last:
            d_attn_in = window(d_attn_in, qkv_sum)
        norm1, inverse1 = layer_stats(tokens_in[index].astype(jnp.float32))
        grad_shift1.append(jnp.sum(d_attn_in, 0))
        grad_scale1.append(jnp.sum(d_attn_in * norm1, 0))
        local = d_mid[index] + norm_back(d_attn_in * (1.0 + scale1[index]), norm1, inverse1)
        local = local.astype(jnp.bfloat16).reshape(GROUPS, row_count, model_width)
        if last:
            for _ in range(3):
                local = window(local, qkv_sum)
            qkv_rows_flow = Flow(gathered(qkv_sum.result))
        else:
            flows = (fc1_sum, proj_sum, biases)
            (local, d_attended[index + 1], qkv_local) = window(
                (local, d_attended[index + 1], qkv_local), *(flows if index == 0 else ())
            )
        returned.append(Flow(sent(local, exchange)))
        if index == 0:
            later_rows_flow = Flow(gathered(fc1_sum.result, proj_sum.result))
    returned[-1].advance(returned[-1].values)
    qkv_rows_flow.advance(qkv_rows_flow.values)
    grad_tokens = merge_latents([flow.result for flow in returned], jnp.float32)
    output = jnp.transpose(out_flow.result, (2, 0, 1, 3)).reshape(
        row_count, group_latents, model_width
    )
    grad_fc2 = fc2_rows_flow.result[0].reshape(hidden, model_width).astype(jnp.float32)
    grad_fc1 = later_rows_flow.result[0].reshape(hidden, model_width).astype(jnp.float32).T
    grad_proj = later_rows_flow.result[1].reshape(width, model_width).astype(jnp.float32)
    grad_qkv = jnp.transpose(
        qkv_rows_flow.result[0].reshape(SHARES, 3, slot, model_width).astype(jnp.float32), (3, 1, 0, 2)
    ).reshape(model_width, 3, width)

    d_modulation = jnp.stack(
        [
            jnp.stack(grad_shift1, 0),
            jnp.stack(grad_scale1, 0),
            grad_gate1,
            grad_shift2,
            grad_scale2,
            grad_gate2,
        ],
        1,
    ).astype(jnp.bfloat16)
    qkv_true = xor_order(
        qkv_bias_part.reshape(GROUPS, 3, 2, 2, 2, slot), place, (2, 3, 4)
    ).reshape(GROUPS, 3 * width)
    d_mod_parts = d_modulation.reshape(latents, 6, GROUPS, width)
    got = group_send(
        [
            jnp.concatenate(
                [
                    lax.dynamic_index_in_dim(d_mod_parts, me ^ mask, 2, keepdims=False).reshape(
                        latents * 6 * width
                    ),
                    qkv_true[mask].astype(jnp.bfloat16),
                ]
            )
            for mask in range(GROUPS)
        ]
    )
    d_mod_group = jnp.stack([piece[: latents * 6 * width] for piece in got], 0).reshape(
        group_latents, 6 * width
    )
    qkv_group = group_add([piece[latents * 6 * width :] for piece in got]).astype(jnp.bfloat16)

    def member_order(array):
        return xor_order(
            array.reshape(2, 2, latents, model_width), me, (0, 1)
        ).reshape(group_latents, model_width)

    everyone = lax.all_gather(
        jnp.concatenate(
            [d_mod_group, member_order(silu_c), qkv_group.reshape(group_latents, -1)], 1
        ),
        "dp",
        axis=0,
    )
    d_mod_all = everyone[:, :, : 6 * width].reshape(-1, 6 * width)
    silu_all = everyone[:, :, 6 * width : 6 * width + model_width].reshape(-1, model_width)
    grad_qv_bias = jnp.sum(
        everyone[:, :, 6 * width + model_width :].reshape(-1, 3, width).astype(jnp.float32), 0
    )[::2]
    grad_ada_bias = jnp.sum(d_mod_all.astype(jnp.float32), 0).reshape(6, width)
    grad_ada = contract(silu_all, d_mod_all).reshape(model_width, 6, width)
    d_silu = member_order(_nt(d_mod_group, ada_flat).astype(jnp.bfloat16))
    d_silu = group_add(group_send([d_silu] * GROUPS))
    grad_cond = jax.vjp(jax.nn.silu, cond_float)[1](d_silu)[0]
    grad_fc1_bias = biases.result[:hidden]
    grad_fc2_bias = biases.result[hidden : hidden + model_width]
    grad_proj_bias = biases.result[hidden + model_width :]
    return (
        output,
        grad_tokens,
        grad_cond,
        grad_qkv,
        grad_qv_bias,
        grad_proj,
        grad_proj_bias,
        grad_fc1,
        grad_fc1_bias,
        grad_fc2,
        grad_fc2_bias,
        grad_ada,
        grad_ada_bias,
    )


def shards(tokens, cond, cotangent, qkv_weight, *rest):
    even = (
        lax.axis_size("tensor") == GROUPS
        and lax.axis_size("dp") == SHARES
        and tokens.shape[1] % GROUPS == 0
        and qkv_weight.shape[2] == 4 * HD
    )
    program = whole_latents if even else split_heads
    return program(tokens, cond, cotangent, qkv_weight, *rest)


def solution(mesh):
    return jax.shard_map(
        shards,
        mesh=mesh,
        in_specs=(
            P("tensor", "dp", None),
            P("dp", None),
            P("tensor", "dp", None),
            P(None, None, "tensor"),
            P(None, "tensor"),
            P("tensor", None),
            P(),
            P(None, "tensor"),
            P("tensor"),
            P("tensor", None),
            P(),
            P(None, None, "tensor"),
            P(None, "tensor"),
        ),
        out_specs=(
            P("tensor", "dp", None),
            P("tensor", "dp", None),
            P("dp", None),
            P(None, None, "tensor"),
            P(None, "tensor"),
            P("tensor", None),
            P(),
            P(None, "tensor"),
            P("tensor"),
            P("tensor", None),
            P(),
            P(None, None, "tensor"),
            P(None, "tensor"),
        ),
        check_vma=False,
    )
```
